32 devices in a mesh: tile: 8 (over z, x), func: 4 (over y, core).
Axes of the slice: x: 2, y: 2, z: 4, core: 2. Of those that a mesh axis runs over, the one named last changes fastest.
Arguments:
- seeds: float32 [12, 5, 256, 128], P('func', None, 'tile'), may hold values from -6 to 6
- checkpoints: float32 [2, 5, 256, 128], P(None, None, ('tile', 'func')), may hold values from -0.6 to 4.2, as said below
Outputs:
- adjoint_start: float32 [12, 5, 256, 128], P('func', None, 'tile')
The draws below stay inside these ranges and needn't reach their ends.
Inputs may be any that keep to these rules, and one draw needn't show every extreme that they name: `checkpoints`: each checkpoint cell is a state with density between 1 and 1.5, each velocity component between -0.4 and 0.4, and pressure between 1 and 1.5.
All inputs are finite; a program needn't handle non-finite values.
Results may differ from the reference program's by a relative error of at most 0.00002.
Values sent between devices are 32-bit elements; how exact they have to be, the bound alone decides.
No kernel may reach another device: no remote copies, remote signals or barrier semaphores. Data moves between devices by JAX's collectives and lax.ppermute only.
A program may use at most 64 MiB of HBM per device.

```python
import jax
import jax.numpy as jnp
from jax import lax

CY = 32
NZ = 4
FIELDS = 5
STEPS = 2
NX = 256
FUNCS = 12


def draw_checkpoints(key, part):
    shape = (STEPS, NX, CY * NZ)
    keys = jax.random.split(key, 5)
    density = jax.random.uniform(keys[0], shape, jnp.float32, 1.0, 1.5)
    speeds = [jnp.clip(0.15 * jax.random.normal(keys[1 + index], shape, jnp.float32), -0.4, 0.4) for index in range(3)]
    press = jax.random.uniform(keys[4], shape, jnp.float32, 1.0, 1.5)
    kinetic = 0.5 * density * (speeds[0] * speeds[0] + speeds[1] * speeds[1] + speeds[2] * speeds[2])
    energy = press / 0.4 + kinetic
    return jnp.stack([density, density * speeds[0], density * speeds[1], density * speeds[2], energy], axis=1)


def block_levels(key, shape, cuts, smallest, largest):
    gain, own = 1.0, jax.random.fold_in(key, 6)
    for dim, parts in cuts:
        heights = jnp.exp(jax.random.uniform(jax.random.fold_in(own, dim), (parts,), jnp.float32, smallest / len(cuts), largest / len(cuts)))
        gain = gain * jnp.repeat(heights, shape[dim] // parts).reshape([-1 if axis == dim else 1 for axis in range(len(shape))])
    return gain


def centred(rng, shape, scale, most, cuts=(), dtype=jnp.bfloat16):
    result = jax.random.normal(rng, shape, jnp.float32) * scale
    if len(cuts) > 0:
        result = block_levels(rng, shape, cuts, -0.22, 0.18) * result
    return jnp.clip(result, min=-most, max=most).astype(dtype)


def setup_inputs(seed: int = 0) -> dict:
    key_of = jax.random.split(jax.random.key(seed), 3)
    seeds = centred(key_of[0], (FUNCS, FIELDS, NX, CY * NZ), 1.0, 6.0, ((0, 4), (2, 8)), jnp.float32)
    checkpoints = draw_checkpoints(jax.random.fold_in(key_of[2], 71), 0)
    return {"seeds": seeds, "checkpoints": checkpoints}


step_size = 0.3

def diff_first(field):
    return (jnp.roll(field, 2, axis=-2) - jnp.roll(field, -2, axis=-2) + 8.0 * (jnp.roll(field, -1, axis=-2) - jnp.roll(field, 1, axis=-2))) / 12.0

def diff_second(field):
    return (jnp.roll(field, 2 * NZ, axis=-1) - jnp.roll(field, -2 * NZ, axis=-1) + 8.0 * (jnp.roll(field, -NZ, axis=-1) - jnp.roll(field, NZ, axis=-1))) / 12.0

def pressure(state):
    density, mom_x, mom_y, mom_z, energy = (state[0], state[1], state[2], state[3], state[4])
    return 0.4 * (energy - (mom_x * mom_x + mom_y * mom_y + mom_z * mom_z) / (2.0 * density))

def flux_first(state):
    density, mom_x, mom_y, mom_z, energy = (state[0], state[1], state[2], state[3], state[4])
    speed = mom_x / density
    press = pressure(state)
    return jnp.stack([mom_x, mom_x * speed + press, mom_y * speed, mom_z * speed, (energy + press) * speed])

def flux_second(state):
    density, mom_x, mom_y, mom_z, energy = (state[0], state[1], state[2], state[3], state[4])
    speed = mom_y / density
    press = pressure(state)
    return jnp.stack([mom_y, mom_x * speed, mom_y * speed + press, mom_z * speed, (energy + press) * speed])

def rhs_field(state):
    return -(diff_first(flux_first(state)) + diff_second(flux_second(state)))

def time_step(state):
    slope_one = rhs_field(state)
    slope_two = rhs_field(state + 0.5 * step_size * slope_one)
    slope_three = rhs_field(state + 0.5 * step_size * slope_two)
    slope_four = rhs_field(state + step_size * slope_three)
    return state + step_size / 6.0 * (slope_one + 2.0 * slope_two + 2.0 * slope_three + slope_four)

def reference(seeds, checkpoints):
    adjoint = seeds
    for moment in reversed(range(STEPS)):
        unused, pullback = jax.vjp(time_step, checkpoints[moment])

        def apply_one(single):
            return pullback(single)[0]
        adjoint = lax.map(apply_one, adjoint)
    return adjoint
```

```python
import jax
import jax.numpy as jnp
from jax import lax
from jax.experimental import pallas as pl
from jax.experimental.pallas import tpu as pltpu
from jax.sharding import PartitionSpec as P

NZ = 4
STEPS = 2
FIELDS = 5
LANES = 128
SUB = 8

step_size = 0.3
twelfth = step_size / 12.0

RIM = 16
BASE_RIM = 24


def swap_near(cells):
    count = lax.axis_size("tile")
    return lax.ppermute(cells, "tile", [(i, i ^ 1) for i in range(count)])


def swap_far(cells):
    count = lax.axis_size("tile")
    pairs = [(i, (i + (1 if i % 2 else -1)) % count) for i in range(count)]
    return lax.ppermute(cells, "tile", pairs)


def turn(cells, places, axis):
    return pltpu.roll(cells, places % cells.shape[axis], axis)


def diff_second(field):
    wide = turn(field, -2 * NZ, 1) - field
    return 8.0 * turn(wide, NZ, 1) - (wide + turn(wide, 2 * NZ, 1))


def diff_first(back_two, back_one, next_one, next_two):
    return 8.0 * (next_one - back_one) - (next_two - back_two)


class Column:
    def __init__(self, load, depth):
        self.load, self.depth, self.held = load, depth, {}

    def __getitem__(self, place):
        if place not in self.held:
            if place < 0:
                cells = turn(self[place + self.depth], 1, 0)
            elif place >= self.depth:
                cells = turn(self[place - self.depth], -1, 0)
            else:
                cells = self.load(place)
            self.held[place] = cells
        return self.held[place]

    def diff(self, place):
        return diff_first(self[place - 2], self[place - 1], self[place + 1], self[place + 2])


def primitives(state):
    density, mom_x, mom_y, mom_z, energy = state
    inverse = 1.0 / density
    vel_x, vel_y, vel_z = mom_x * inverse, mom_y * inverse, mom_z * inverse
    half = 0.5 * (vel_x * vel_x + vel_y * vel_y + vel_z * vel_z)
    press = 0.4 * (energy - density * half)
    total = energy + press
    return vel_x, vel_y, vel_z, total * inverse, half, press, total


def state_stages(moment, base_ref, coef_ref, now_ref, flux_ref, slope_ref, depth):
    def rows(place):
        return pl.ds(place, SUB, stride=depth)

    for stage in range(4):
        for j in range(depth):
            if stage == 0:
                state = [base_ref[moment, k, rows(j), :] for k in range(FIELDS)]
            else:
                state = [now_ref[k, j] for k in range(FIELDS)]
            vel_x, vel_y, vel_z, heat, half, press, total = primitives(state)
            for k, cells in enumerate((vel_x, vel_y, vel_z, heat, half)):
                coef_ref[stage, k, rows(j), :] = cells
            if stage == 3:
                continue
            _, mom_x, mom_y, mom_z, _ = state
            cross = mom_x * vel_y
            first = (mom_x, mom_x * vel_x + press, cross, mom_z * vel_x, total * vel_x)
            second = (mom_y, cross, mom_y * vel_y + press, mom_z * vel_y, total * vel_y)
            for k in range(FIELDS):
                flux_ref[k, j] = first[k]
                slope_ref[k, j] = diff_second(second[k])
        if stage == 3:
            return
        scale = (0.5 if stage < 2 else 1.0) * twelfth
        for k in range(FIELDS):
            column = Column(lambda place, k=k: flux_ref[k, place], depth)
            for j in range(depth):
                slope = column.diff(j) + slope_ref[k, j]
                now_ref[k, j] = base_ref[moment, k, rows(j), :] - scale * slope


def pull_stages(one, coef_ref, adj_ref, acc_ref, hold_ref, depth):
    shift = BASE_RIM - RIM
    for stage in (3, 2, 1, 0):
        source = (adj_ref.at[one], hold_ref.at[0], hold_ref.at[1], hold_ref.at[0])[3 - stage]
        columns = [Column(lambda place, k=k: source[k, place], depth) for k in range(FIELDS)]
        for j in range(depth):
            vel_x, vel_y, vel_z, heat, half = [
                coef_ref[stage, k, pl.ds(shift + j, SUB, stride=depth), :] for k in range(5)
            ]
            a = [column.diff(j) for column in columns]
            b = [diff_second(column[j]) for column in columns]
            mix_x = vel_x * a[1] + vel_y * a[2] + vel_z * a[3] + heat * a[4]
            mix_y = vel_x * b[1] + vel_y * b[2] + vel_z * b[3] + heat * b[4]
            lift = vel_x * a[4] + vel_y * b[4]
            press = 0.4 * (a[1] + b[2] + lift)
            term = (
                half * press - vel_x * mix_x - vel_y * mix_y,
                a[0] + mix_x + vel_x * (a[1] - press) + vel_y * b[1],
                b[0] + mix_y + vel_y * (b[2] - press) + vel_x * a[2],
                vel_x * a[3] + vel_y * b[3] - vel_z * press,
                lift + press,
            )
            for k in range(FIELDS):
                if stage == 3:
                    start = columns[k][j]
                    hold_ref[0, k, j] = start + (0.5 * twelfth) * term[k]
                    acc_ref[k, j] = start + (twelfth / 6.0) * term[k]
                elif stage == 0:
                    adj_ref[one, k, j] = acc_ref[k, j] + (twelfth / 6.0) * term[k]
                else:
                    scale = (0.5 if stage == 2 else 1.0) * twelfth
                    hold_ref[1 if stage == 2 else 0, k, j] = adj_ref[one, k, j] + scale * term[k]
                    acc_ref[k, j] = acc_ref[k, j] + (twelfth / 3.0) * term[k]


def kernel(
    seeds_ref, near_ref, far_ref, blocks_ref, out_ref,
    wide_ref, adj_ref, acc_ref, hold_ref, base_ref, coef_ref, now_ref, flux_ref, slope_ref,
):
    funcs, _, strip, _ = seeds_ref.shape
    spread, _, block, _ = blocks_ref.shape
    tall = strip + 2 * RIM
    depth, base_depth = tall // SUB, (strip + 2 * BASE_RIM) // SUB
    even = lax.rem(lax.axis_index("tile"), 2) == 0

    def lay(left_ref, right_ref, left_part, right_part):
        for one in range(funcs):
            for k in range(FIELDS):
                wide_ref[one, k, :RIM, :] = left_ref[one, k]
                wide_ref[one, k, RIM + strip :, :] = right_ref[one, k]
        for owner in range(spread):
            start = owner * block
            for moment in range(STEPS):
                for k in range(FIELDS):
                    field = moment * FIELDS + k
                    if start >= strip - BASE_RIM:
                        place = start - (strip - BASE_RIM)
                        base_ref[moment, k, place : place + block, :] = blocks_ref[owner, left_part * STEPS * FIELDS + field]
                    if start + block <= BASE_RIM:
                        place = BASE_RIM + strip + start
                        base_ref[moment, k, place : place + block, :] = blocks_ref[owner, right_part * STEPS * FIELDS + field]

    pl.when(even)(lambda: lay(far_ref, near_ref, 2, 1))
    pl.when(jnp.logical_not(even))(lambda: lay(near_ref, far_ref, 1, 2))
    for one in range(funcs):
        for k in range(FIELDS):
            wide_ref[one, k, RIM : RIM + strip, :] = seeds_ref[one, k]
    for owner in range(spread):
        place = BASE_RIM + owner * block
        for moment in range(STEPS):
            for k in range(FIELDS):
                base_ref[moment, k, place : place + block, :] = blocks_ref[owner, moment * FIELDS + k]
    for one in range(funcs):
        for k in range(FIELDS):
            for j in range(depth):
                adj_ref[one, k, j] = wide_ref[one, k, pl.ds(j, SUB, stride=depth), :]

    def one_step(index, carry):
        moment = STEPS - 1 - index
        state_stages(moment, base_ref, coef_ref, now_ref, flux_ref, slope_ref, base_depth)

        def one_func(one, inner):
            pull_stages(one, coef_ref, adj_ref, acc_ref, hold_ref, depth)
            return inner

        return lax.fori_loop(0, funcs, one_func, carry)

    lax.fori_loop(0, STEPS, one_step, 0)
    for one in range(funcs):
        for k in range(FIELDS):
            for j in range(depth):
                wide_ref[one, k, pl.ds(j, SUB, stride=depth), :] = adj_ref[one, k, j]
            out_ref[one, k] = wide_ref[one, k, RIM : RIM + strip, :]


def local(seeds, checkpoints):
    funcs, _, strip, _ = seeds.shape
    block = checkpoints.shape[2]
    even = lax.rem(lax.axis_index("tile"), 2) == 0
    own = checkpoints.reshape(STEPS * FIELDS, block, LANES)
    far_base, near_base = swap_far(own), swap_near(own)
    tail = strip - RIM
    far_edge = lax.dynamic_slice_in_dim(seeds, jnp.where(even, 0, tail), RIM, axis=2)
    near_edge = lax.dynamic_slice_in_dim(seeds, jnp.where(even, tail, 0), RIM, axis=2)
    far, near = swap_far(far_edge), swap_near(near_edge)
    blocks = lax.all_gather(jnp.concatenate([own, near_base, far_base], axis=0), "func", axis=0, tiled=False)
    tall, base_tall = strip + 2 * RIM, strip + 2 * BASE_RIM
    depth, base_depth = tall // SUB, base_tall // SUB
    shapes = [
        (funcs, FIELDS, tall, LANES),
        (funcs, FIELDS, depth, SUB, LANES),
        (FIELDS, depth, SUB, LANES),
        (2, FIELDS, depth, SUB, LANES),
        (STEPS, FIELDS, base_tall, LANES),
        (4, 5, base_tall, LANES),
        (FIELDS, base_depth, SUB, LANES),
        (FIELDS, base_depth, SUB, LANES),
        (FIELDS, base_depth, SUB, LANES),
    ]
    vmem = pl.BlockSpec(memory_space=pltpu.VMEM)
    return pl.pallas_call(
        kernel,
        out_shape=jax.ShapeDtypeStruct(seeds.shape, jnp.float32),
        in_specs=[vmem] * 4,
        out_specs=vmem,
        scratch_shapes=[pltpu.VMEM(shape, jnp.float32) for shape in shapes],
        compiler_params=pltpu.CompilerParams(vmem_limit_bytes=32 * 1024 * 1024),
        name="two_steps",
    )(seeds, near, far, blocks)


def solution(mesh):
    return jax.shard_map(
        local,
        mesh=mesh,
        in_specs=(P("func", None, "tile", None), P(None, None, ("tile", "func"), None)),
        out_specs=P("func", None, "tile", None),
        check_vma=False,
    )
```

```python
import jax
import jax.numpy as jnp
from jax import lax
from jax.experimental import pallas as pl
from jax.experimental.pallas import tpu as pltpu
from jax.sharding import PartitionSpec as P

NZ = 4
STEPS = 2
FIELDS = 5
LANES = 128
SUB = 8

step_size = 0.3
twelfth = step_size / 12.0

RIM = 16
BASE_RIM = 24


def swap_near(cells):
    count = lax.axis_size("tile")
    return lax.ppermute(cells, "tile", [(i, i ^ 1) for i in range(count)])


def swap_far(cells):
    count = lax.axis_size("tile")
    pairs = [(i, (i + (1 if i % 2 else -1)) % count) for i in range(count)]
    return lax.ppermute(cells, "tile", pairs)


def turn(cells, places, axis):
    return pltpu.roll(cells, places % cells.shape[axis], axis)


def second_weights():
    shape = (LANES, LANES)
    ahead = lax.broadcasted_iota(jnp.int32, shape, 0) - lax.broadcasted_iota(jnp.int32, shape, 1)
    ahead = jnp.bitwise_and(ahead, LANES - 1)
    weights = jnp.zeros(shape, jnp.float32)
    for places, weight in ((NZ, 8.0), (-NZ, -8.0), (2 * NZ, -1.0), (-2 * NZ, 1.0)):
        weights = jnp.where(ahead == places % LANES, weight, weights)
    return jnp.concatenate([weights, weights], axis=0).astype(jnp.bfloat16)


def diff_second(cells, weights):
    high = cells.astype(jnp.bfloat16)
    low = (cells - high.astype(jnp.float32)).astype(jnp.bfloat16)
    return jnp.dot(jnp.concatenate([high, low], axis=1), weights, preferred_element_type=jnp.float32)


def diff_first(back_two, back_one, next_one, next_two):
    return 8.0 * (next_one - back_one) - (next_two - back_two)


class Column:
    def __init__(self, load, depth):
        self.load, self.depth, self.held = load, depth, {}

    def __getitem__(self, place):
        if place not in self.held:
            if place < 0:
                cells = turn(self[place + self.depth], 1, 0)
            elif place >= self.depth:
                cells = turn(self[place - self.depth], -1, 0)
            else:
                cells = self.load(place)
            self.held[place] = cells
        return self.held[place]

    def diff(self, place):
        return diff_first(self[place - 2], self[place - 1], self[place + 1], self[place + 2])


def primitives(state):
    density, mom_x, mom_y, mom_z, energy = state
    inverse = 1.0 / density
    vel_x, vel_y, vel_z = mom_x * inverse, mom_y * inverse, mom_z * inverse
    half = 0.5 * (vel_x * vel_x + vel_y * vel_y + vel_z * vel_z)
    press = 0.4 * (energy - density * half)
    total = energy + press
    return vel_x, vel_y, vel_z, total * inverse, half, press, total


def tile(place):
    return slice(place * SUB, (place + 1) * SUB)


def state_stages(base_ref, coef_ref, now_ref, flux_ref, slope_ref, weights, depth):
    tall = depth * SUB

    def rows(place):
        return pl.ds(place, SUB, stride=depth)

    for stage in range(4):
        for moment in range(STEPS):
            for j in range(depth):
                if stage == 0:
                    state = [base_ref[moment, k, rows(j), :] for k in range(FIELDS)]
                else:
                    state = [now_ref[moment, k, tile(j)] for k in range(FIELDS)]
                vel_x, vel_y, vel_z, heat, half, press, total = primitives(state)
                for k, cells in enumerate((vel_x, vel_y, vel_z, heat, half)):
                    coef_ref[moment, stage, k, rows(j), :] = cells
                if stage == 3:
                    continue
                _, mom_x, mom_y, mom_z, _ = state
                cross = mom_x * vel_y
                first = (mom_x, mom_x * vel_x + press, cross, mom_z * vel_x, total * vel_x)
                second = (mom_y, cross, mom_y * vel_y + press, mom_z * vel_y, total * vel_y)
                for k in range(FIELDS):
                    flux_ref[moment, k, tile(j)] = first[k]
                    slope_ref[moment, k, tile(j)] = second[k]
            if stage == 3:
                continue
            second = diff_second(slope_ref[moment].reshape(FIELDS * tall, LANES), weights)
            slope_ref[moment] = second.reshape(FIELDS, tall, LANES)
        if stage == 3:
            return
        scale = (0.5 if stage < 2 else 1.0) * twelfth
        for moment in range(STEPS):
            for k in range(FIELDS):
                column = Column(lambda place, k=k: flux_ref[moment, k, tile(place)], depth)
                for j in range(depth):
                    slope = column.diff(j) + slope_ref[moment, k, tile(j)]
                    now_ref[moment, k, tile(j)] = base_ref[moment, k, rows(j), :] - scale * slope


def pull_stages(moment, coef_ref, adj_ref, acc_ref, hold_ref, second_ref, weights, depth):
    shift = BASE_RIM - RIM
    funcs, tall = adj_ref.shape[0], depth * SUB
    for stage in (3, 2, 1, 0):
        source_ref = (adj_ref, hold_ref.at[0], hold_ref.at[1], hold_ref.at[0])[3 - stage]

        def second_of(one):
            second = diff_second(source_ref[one].reshape(FIELDS * tall, LANES), weights)
            second_ref[one] = second.reshape(FIELDS, tall, LANES)

        second_of(0)
        for one in range(funcs):
            if one + 1 < funcs:
                second_of(one + 1)
            columns = [Column(lambda place, k=k: source_ref[one, k, tile(place)], depth) for k in range(FIELDS)]
            for j in range(depth):
                vel_x, vel_y, vel_z, heat, half = [
                    coef_ref[moment, stage, k, pl.ds(shift + j, SUB, stride=depth), :] for k in range(5)
                ]
                a = [column.diff(j) for column in columns]
                b = [second_ref[one, k, tile(j)] for k in range(FIELDS)]
                mix_x = vel_x * a[1] + vel_y * a[2] + vel_z * a[3] + heat * a[4]
                mix_y = vel_x * b[1] + vel_y * b[2] + vel_z * b[3] + heat * b[4]
                lift = vel_x * a[4] + vel_y * b[4]
                press = 0.4 * (a[1] + b[2] + lift)
                term = (
                    half * press - vel_x * mix_x - vel_y * mix_y,
                    a[0] + mix_x + vel_x * (a[1] - press) + vel_y * b[1],
                    b[0] + mix_y + vel_y * (b[2] - press) + vel_x * a[2],
                    vel_x * a[3] + vel_y * b[3] - vel_z * press,
                    lift + press,
                )
                for k in range(FIELDS):
                    if stage == 3:
                        start = columns[k][j]
                        hold_ref[0, one, k, tile(j)] = start + (0.5 * twelfth) * term[k]
                        acc_ref[one, k, tile(j)] = start + (twelfth / 6.0) * term[k]
                    elif stage == 0:
                        adj_ref[one, k, tile(j)] = acc_ref[one, k, tile(j)] + (twelfth / 6.0) * term[k]
                    else:
                        scale = (0.5 if stage == 2 else 1.0) * twelfth
                        place = 1 if stage == 2 else 0
                        hold_ref[place, one, k, tile(j)] = adj_ref[one, k, tile(j)] + scale * term[k]
                        acc_ref[one, k, tile(j)] = acc_ref[one, k, tile(j)] + (twelfth / 3.0) * term[k]


def kernel(
    seeds_ref, near_ref, far_ref, blocks_ref, out_ref,
    wide_ref, adj_ref, acc_ref, hold_ref, second_ref, base_ref, coef_ref, now_ref, flux_ref, slope_ref,
):
    funcs, _, strip, _ = seeds_ref.shape
    spread, _, block, _ = blocks_ref.shape
    tall = strip + 2 * RIM
    depth, base_depth = tall // SUB, (strip + 2 * BASE_RIM) // SUB
    even = lax.rem(lax.axis_index("tile"), 2) == 0

    def lay(left_ref, right_ref, left_part, right_part):
        for one in range(funcs):
            for k in range(FIELDS):
                wide_ref[one, k, :RIM, :] = left_ref[one, k]
                wide_ref[one, k, RIM + strip :, :] = right_ref[one, k]
        for owner in range(spread):
            start = owner * block
            for moment in range(STEPS):
                for k in range(FIELDS):
                    field = moment * FIELDS + k
                    if start >= strip - BASE_RIM:
                        place = start - (strip - BASE_RIM)
                        base_ref[moment, k, place : place + block, :] = blocks_ref[owner, left_part * STEPS * FIELDS + field]
                    if start + block <= BASE_RIM:
                        place = BASE_RIM + strip + start
                        base_ref[moment, k, place : place + block, :] = blocks_ref[owner, right_part * STEPS * FIELDS + field]

    pl.when(even)(lambda: lay(far_ref, near_ref, 2, 1))
    pl.when(jnp.logical_not(even))(lambda: lay(near_ref, far_ref, 1, 2))
    for one in range(funcs):
        for k in range(FIELDS):
            wide_ref[one, k, RIM : RIM + strip, :] = seeds_ref[one, k]
    for owner in range(spread):
        place = BASE_RIM + owner * block
        for moment in range(STEPS):
            for k in range(FIELDS):
                base_ref[moment, k, place : place + block, :] = blocks_ref[owner, moment * FIELDS + k]
    for one in range(funcs):
        for k in range(FIELDS):
            for j in range(depth):
                adj_ref[one, k, tile(j)] = wide_ref[one, k, pl.ds(j, SUB, stride=depth), :]

    weights = second_weights()
    state_stages(base_ref, coef_ref, now_ref, flux_ref, slope_ref, weights, base_depth)

    def one_step(index, carry):
        moment = STEPS - 1 - index
        pull_stages(moment, coef_ref, adj_ref, acc_ref, hold_ref, second_ref, weights, depth)
        return carry

    lax.fori_loop(0, STEPS, one_step, 0)
    for one in range(funcs):
        for k in range(FIELDS):
            for j in range(depth):
                wide_ref[one, k, pl.ds(j, SUB, stride=depth), :] = adj_ref[one, k, tile(j)]
            out_ref[one, k] = wide_ref[one, k, RIM : RIM + strip, :]


def local(seeds, checkpoints):
    funcs, _, strip, _ = seeds.shape
    block = checkpoints.shape[2]
    even = lax.rem(lax.axis_index("tile"), 2) == 0
    own = checkpoints.reshape(STEPS * FIELDS, block, LANES)
    far_base, near_base = swap_far(own), swap_near(own)
    tail = strip - RIM
    far_edge = lax.dynamic_slice_in_dim(seeds, jnp.where(even, 0, tail), RIM, axis=2)
    near_edge = lax.dynamic_slice_in_dim(seeds, jnp.where(even, tail, 0), RIM, axis=2)
    far, near = swap_far(far_edge), swap_near(near_edge)
    blocks = lax.all_gather(jnp.concatenate([own, near_base, far_base], axis=0), "func", axis=0, tiled=False)
    tall, base_tall = strip + 2 * RIM, strip + 2 * BASE_RIM
    shapes = [
        (funcs, FIELDS, tall, LANES),
        (funcs, FIELDS, tall, LANES),
        (funcs, FIELDS, tall, LANES),
        (2, funcs, FIELDS, tall, LANES),
        (funcs, FIELDS, tall, LANES),
        (STEPS, FIELDS, base_tall, LANES),
        (STEPS, 4, 5, base_tall, LANES),
        (STEPS, FIELDS, base_tall, LANES),
        (STEPS, FIELDS, base_tall, LANES),
        (STEPS, FIELDS, base_tall, LANES),
    ]
    vmem = pl.BlockSpec(memory_space=pltpu.VMEM)
    return pl.pallas_call(
        kernel,
        out_shape=jax.ShapeDtypeStruct(seeds.shape, jnp.float32),
        in_specs=[vmem] * 4,
        out_specs=vmem,
        scratch_shapes=[pltpu.VMEM(shape, jnp.float32) for shape in shapes],
        compiler_params=pltpu.CompilerParams(vmem_limit_bytes=32 * 1024 * 1024),
        name="two_steps",
    )(seeds, near, far, blocks)


def solution(mesh):
    return jax.shard_map(
        local,
        mesh=mesh,
        in_specs=(P("func", None, "tile", None), P(None, None, ("tile", "func"), None)),
        out_specs=P("func", None, "tile", None),
        check_vma=False,
    )
```

```python
import jax
import jax.numpy as jnp
from jax import lax
from jax.experimental import pallas as pl
from jax.experimental.pallas import tpu as pltpu
from jax.sharding import PartitionSpec as P

NZ = 4
STEPS = 2
FIELDS = 5
LANES = 128
SUB = 8

step_size = 0.3
twelfth = step_size / 12.0

RIM = 16
BASE_RIM = 24
LONG_RIM = 20
SHORT_RIM = 12
STATE_RIMS = (SHORT_RIM, LONG_RIM)
STILL = (1.0, 0.0, 0.0, 0.0, 2.5)
STATE_EDGES = ((8, 8, 16, 16), (0, 0, 8, 8))


def swap_near(cells):
    count = lax.axis_size("tile")
    return lax.ppermute(cells, "tile", [(i, i ^ 1) for i in range(count)])


def swap_far(cells):
    count = lax.axis_size("tile")
    pairs = [(i, (i + (1 if i % 2 else -1)) % count) for i in range(count)]
    return lax.ppermute(cells, "tile", pairs)


def second_weights():
    shape = (LANES, LANES)
    ahead = lax.broadcasted_iota(jnp.int32, shape, 0) - lax.broadcasted_iota(jnp.int32, shape, 1)
    ahead = jnp.bitwise_and(ahead, LANES - 1)
    weights = jnp.zeros(shape, jnp.float32)
    for places, weight in ((NZ, 8.0), (-NZ, -8.0), (2 * NZ, -1.0), (-2 * NZ, 1.0)):
        weights = jnp.where(ahead == places % LANES, weight, weights)
    return jnp.concatenate([weights, weights], axis=0).astype(jnp.bfloat16)


def first_weights(count, total, skip):
    shape = (count, 2 * total)
    column = lax.broadcasted_iota(jnp.int32, shape, 1)
    column = jnp.where(column < total, column, column - total)
    ahead = column - lax.broadcasted_iota(jnp.int32, shape, 0) - skip
    weights = jnp.zeros(shape, jnp.float32)
    for places, weight in ((1, 8.0), (-1, -8.0), (2, -1.0), (-2, 1.0)):
        weights = jnp.where(ahead == places, weight, weights)
    return weights.astype(jnp.bfloat16)


def parts(cells):
    high = cells.astype(jnp.bfloat16)
    return high, (cells - high.astype(jnp.float32)).astype(jnp.bfloat16)


def second_diff(high, low, weights):
    fields, count, _ = high.shape
    cells = jnp.concatenate([high, low], axis=2).reshape(fields * count, 2 * LANES)
    return jnp.dot(cells, weights, preferred_element_type=jnp.float32)


def first_diff(high, low, weights):
    cells = jnp.concatenate([high, low], axis=1)
    cells = jnp.concatenate([cells[k] for k in range(FIELDS)], axis=1)
    return jnp.dot(weights, cells, preferred_element_type=jnp.float32)


def lanes(k):
    return slice(k * LANES, (k + 1) * LANES)


def primitives(state):
    density, mom_x, mom_y, mom_z, energy = state
    inverse = 1.0 / density
    vel_x, vel_y, vel_z = mom_x * inverse, mom_y * inverse, mom_z * inverse
    half = 0.5 * (vel_x * vel_x + vel_y * vel_y + vel_z * vel_z)
    press = 0.4 * (energy - density * half)
    total = energy + press
    return vel_x, vel_y, vel_z, total * inverse, half, press, total


def tiles(start, stop):
    return [slice(place, place + SUB) for place in range(start, stop, SUB)]


def within(cells, rows, edge, span, k):
    if edge <= rows.start and rows.stop <= span - edge:
        return cells
    place = rows.start + lax.broadcasted_iota(jnp.int32, cells.shape, 0)
    return jnp.where(jnp.logical_and(place >= edge, place < span - edge), cells, STILL[k])


def state_stages(base_ref, coef_ref, now_ref, flux_ref, slope_ref, first_ref, second_ref, lefts, weights, span):
    for stage in range(4):
        for moment in range(STEPS):
            here, there = STATE_EDGES[moment][stage], STATE_EDGES[moment][min(stage + 1, 3)]
            for rows in tiles(here, span - here):
                source_ref = base_ref if stage == 0 else now_ref
                state = [source_ref[moment, k, rows] for k in range(FIELDS)]
                vel_x, vel_y, vel_z, heat, half, press, total = primitives(state)
                for k, cells in enumerate((vel_x, vel_y, vel_z, heat, half)):
                    coef_ref[moment, stage, k, rows] = cells
                if stage == 3:
                    continue
                _, mom_x, mom_y, mom_z, _ = state
                cross = mom_x * vel_y
                first = (mom_x, mom_x * vel_x + press, cross, mom_z * vel_x, total * vel_x)
                second = (mom_y, cross, mom_y * vel_y + press, mom_z * vel_y, total * vel_y)
                for k in range(FIELDS):
                    flux_ref[moment, k, rows] = first[k]
                    if there <= rows.start < span - there:
                        slope_ref[moment, k, rows] = second[k]
            if stage == 3:
                continue
            count, total_rows = span - 2 * there, span - 2 * here
            left = lefts[count, total_rows]
            flux = flux_ref[moment, :, here : span - here]
            first_ref[moment, there : span - there] = first_diff(*parts(flux), left)
            slope = slope_ref[moment, :, there : span - there]
            second = second_diff(*parts(slope), weights)
            second_ref[moment, :, there : span - there] = second.reshape(FIELDS, count, LANES)
        if stage == 3:
            return
        scale = (0.5 if stage < 2 else 1.0) * twelfth
        for moment in range(STEPS):
            there = STATE_EDGES[moment][stage + 1]
            for k in range(FIELDS):
                for rows in tiles(there, span - there):
                    slope = first_ref[moment, rows, lanes(k)] + second_ref[moment, k, rows]
                    cells = base_ref[moment, k, rows] - scale * slope
                    now_ref[moment, k, rows] = within(cells, rows, BASE_RIM - STATE_RIMS[moment] + 2 * (stage + 1), span, k)


def pull_stages(moment, coef_ref, adj_ref, hold_ref, first_ref, second_ref, out_ref, lefts, weights):
    funcs, _, tall, _ = adj_ref.shape
    shift, last = BASE_RIM - RIM, moment == 0
    start = (STEPS - 1 - moment) * SUB
    for stage in (3, 2, 1, 0):
        edge = start + SUB if stage == 0 else start
        source_ref = adj_ref if stage == 3 else hold_ref.at[2 - stage]
        total = tall - 2 * start
        left = lefts[tall - 2 * edge, total]

        def differences(one):
            high, low = parts(source_ref[one, :, start : tall - start])
            first_ref[one, edge : tall - edge] = first_diff(high, low, left)
            second = second_diff(high, low, weights)
            second_ref[one, :, start : tall - start] = second.reshape(FIELDS, total, LANES)

        differences(0)
        for one in range(funcs):
            if one + 1 < funcs:
                differences(one + 1)
            for rows in tiles(edge, tall - edge):
                base_rows = slice(rows.start + shift, rows.stop + shift)
                vel_x, vel_y, vel_z, heat, half = [coef_ref[moment, stage, k, base_rows] for k in range(5)]
                a = [first_ref[one, rows, lanes(k)] for k in range(FIELDS)]
                b = [second_ref[one, k, rows] for k in range(FIELDS)]
                mix_x = vel_x * a[1] + vel_y * a[2] + vel_z * a[3] + heat * a[4]
                mix_y = vel_x * b[1] + vel_y * b[2] + vel_z * b[3] + heat * b[4]
                lift = vel_x * a[4] + vel_y * b[4]
                press = 0.4 * (a[1] + b[2] + lift)
                term = (
                    half * press - vel_x * mix_x - vel_y * mix_y,
                    a[0] + mix_x + vel_x * (a[1] - press) + vel_y * b[1],
                    b[0] + mix_y + vel_y * (b[2] - press) + vel_x * a[2],
                    vel_x * a[3] + vel_y * b[3] - vel_z * press,
                    lift + press,
                )
                for k in range(FIELDS):
                    adj = adj_ref[one, k, rows]
                    if stage > 0:
                        scale = (1.0 if stage == 1 else 0.5) * twelfth
                        hold_ref[3 - stage, one, k, rows] = adj + scale * term[k]
                        continue
                    one_third, two_thirds, rest = [hold_ref[place, one, k, rows] for place in range(3)]
                    mean = (one_third - adj + rest + 2.0 * two_thirds) * (1.0 / 3.0)
                    result = mean + (twelfth / 6.0) * term[k]
                    if last:
                        out_ref[one, k, rows.start - RIM : rows.stop - RIM] = result
                    else:
                        adj_ref[one, k, rows] = result


def kernel(
    seeds_ref, near_ref, far_ref, blocks_ref, out_ref,
    adj_ref, hold_ref, first_ref, second_ref,
    base_ref, coef_ref, now_ref, flux_ref, slope_ref, base_first_ref, base_second_ref,
):
    funcs, _, strip, _ = seeds_ref.shape
    spread, _, block, _ = blocks_ref.shape
    tall, span = strip + 2 * RIM, strip + 2 * BASE_RIM
    even = lax.rem(lax.axis_index("tile"), 2) == 0

    def lay(left_ref, right_ref):
        for one in range(funcs):
            for k in range(FIELDS):
                adj_ref[one, k, :RIM] = left_ref[one, k]
                adj_ref[one, k, RIM + strip :] = right_ref[one, k]

    def lay_base(part, moment, shift, low, high):
        for owner in range(spread):
            start, stop = max(low, owner * block), min(high, (owner + 1) * block)
            if start < stop:
                rows = slice(start - owner * block, stop - owner * block)
                place = BASE_RIM + shift + start
                for k in range(FIELDS):
                    base_ref[moment, k, place : place + stop - start, :] = blocks_ref[owner, part * FIELDS + k, rows, :]

    for moment in range(STEPS):
        edge = BASE_RIM - STATE_RIMS[moment]
        for start in (STATE_EDGES[moment][0], span - STATE_EDGES[moment][0] - SUB):
            if start < edge or start + SUB > span - edge:
                for k in range(FIELDS):
                    base_ref[moment, k, start : start + SUB] = jnp.full((SUB, LANES), STILL[k], jnp.float32)
    middle = strip // 2
    lay_base(0, 0, 0, 0, strip)
    lay_base(1, 1, 0, 0, strip)
    lay_base(2, 1, strip, 0, middle)
    lay_base(2, 1, -strip, middle, strip)
    lay_base(3, 0, strip, 0, SHORT_RIM)
    lay_base(3, 1, -strip, max(SHORT_RIM, strip - LONG_RIM), middle)
    lay_base(3, 1, strip, middle, min(LONG_RIM, strip - SHORT_RIM))
    lay_base(3, 0, -strip, strip - SHORT_RIM, strip)

    weights = second_weights()
    sizes = {(tall - 2 * start, tall - 2 * start) for start in range(0, STEPS * SUB, SUB)}
    sizes |= {(tall - 2 * start - 2 * SUB, tall - 2 * start) for start in range(0, STEPS * SUB, SUB)}
    for edges in STATE_EDGES:
        sizes |= {(span - 2 * edges[n + 1], span - 2 * edges[n]) for n in range(3)}
    lefts = {size: first_weights(*size, (size[1] - size[0]) // 2) for size in sorted(sizes)}
    state_stages(
        base_ref, coef_ref, now_ref, flux_ref, slope_ref, base_first_ref, base_second_ref, lefts, weights, span
    )
    pl.when(even)(lambda: lay(far_ref, near_ref))
    pl.when(jnp.logical_not(even))(lambda: lay(near_ref, far_ref))
    for one in range(funcs):
        for k in range(FIELDS):
            adj_ref[one, k, RIM : RIM + strip] = seeds_ref[one, k]
    for moment in reversed(range(STEPS)):
        pull_stages(moment, coef_ref, adj_ref, hold_ref, first_ref, second_ref, out_ref, lefts, weights)


def local(seeds, checkpoints):
    funcs, _, strip, _ = seeds.shape
    block = checkpoints.shape[2]
    even = lax.rem(lax.axis_index("tile"), 2) == 0
    far_base, near_base = swap_far(checkpoints), swap_near(checkpoints)
    tail = strip - RIM
    far_edge = lax.dynamic_slice_in_dim(seeds, jnp.where(even, 0, tail), RIM, axis=2)
    near_edge = lax.dynamic_slice_in_dim(seeds, jnp.where(even, tail, 0), RIM, axis=2)
    far, near = swap_far(far_edge), swap_near(near_edge)
    lower = lax.axis_index("func") * block < strip // 2
    take_far = even != lower
    main = lax.select(take_far, far_base, near_base)
    other = lax.select(take_far, near_base[1], far_base[1])
    place = lax.axis_index("func") * block + lax.broadcasted_iota(jnp.int32, (1, block, 1), 1)
    inner = jnp.logical_and(place >= SHORT_RIM, place < strip - SHORT_RIM)
    rest = jnp.where(inner, other, main[0])
    own = checkpoints.reshape(STEPS * FIELDS, block, LANES)
    packed = jnp.concatenate([own, main[1], rest], axis=0)
    blocks = lax.all_gather(packed, "func", axis=0, tiled=False)
    tall, span = strip + 2 * RIM, strip + 2 * BASE_RIM
    shapes = [
        (funcs, FIELDS, tall, LANES),
        (3, funcs, FIELDS, tall, LANES),
        (funcs, tall, FIELDS * LANES),
        (funcs, FIELDS, tall, LANES),
        (STEPS, FIELDS, span, LANES),
        (STEPS, 4, 5, span, LANES),
        (STEPS, FIELDS, span, LANES),
        (STEPS, FIELDS, span, LANES),
        (STEPS, FIELDS, span, LANES),
        (STEPS, span, FIELDS * LANES),
        (STEPS, FIELDS, span, LANES),
    ]
    vmem = pl.BlockSpec(memory_space=pltpu.VMEM)
    return pl.pallas_call(
        kernel,
        out_shape=jax.ShapeDtypeStruct(seeds.shape, jnp.float32),
        in_specs=[vmem] * 4,
        out_specs=vmem,
        scratch_shapes=[pltpu.VMEM(shape, jnp.float32) for shape in shapes],
        compiler_params=pltpu.CompilerParams(vmem_limit_bytes=32 * 1024 * 1024),
        name="two_steps",
    )(seeds, near, far, blocks)


def solution(mesh):
    return jax.shard_map(
        local,
        mesh=mesh,
        in_specs=(P("func", None, "tile", None), P(None, None, ("tile", "func"), None)),
        out_specs=P("func", None, "tile", None),
        check_vma=False,
    )
```

```python
from itertools import chain

import jax
import jax.numpy as jnp
from jax import lax
from jax.experimental import pallas as pl
from jax.experimental.pallas import tpu as pltpu
from jax.sharding import PartitionSpec as P

NZ = 4
STEPS = 2
FIELDS = 5
LANES = 128
SUB = 8

step_size = 0.3
twelfth = step_size / 12.0

RIM = 16
BASE_RIM = 24
LONG_RIM = 20
SHORT_RIM = 12
STATE_RIMS = (SHORT_RIM, LONG_RIM)
START_EVERY, STORES = 2, 2
STILL = (1.0, 0.0, 0.0, 0.0, 2.5)
STATE_EDGES = ((8, 8, 16, 16), (0, 0, 8, 8))


def swap_near(cells):
    count = lax.axis_size("tile")
    return lax.ppermute(cells, "tile", [(i, i ^ 1) for i in range(count)])


def swap_far(cells):
    count = lax.axis_size("tile")
    pairs = [(i, (i + (1 if i % 2 else -1)) % count) for i in range(count)]
    return lax.ppermute(cells, "tile", pairs)


def second_weights():
    shape = (LANES, LANES)
    ahead = lax.broadcasted_iota(jnp.int32, shape, 0) - lax.broadcasted_iota(jnp.int32, shape, 1)
    ahead = jnp.bitwise_and(ahead, LANES - 1)
    weights = jnp.zeros(shape, jnp.float32)
    for places, weight in ((NZ, 8.0), (-NZ, -8.0), (2 * NZ, -1.0), (-2 * NZ, 1.0)):
        weights = jnp.where(ahead == places % LANES, weight, weights)
    return jnp.concatenate([weights, weights], axis=0).astype(jnp.bfloat16)


def first_weights(count, total, skip):
    shape = (count, 2 * total)
    column = lax.broadcasted_iota(jnp.int32, shape, 1)
    column = jnp.where(column < total, column, column - total)
    ahead = column - lax.broadcasted_iota(jnp.int32, shape, 0) - skip
    weights = jnp.zeros(shape, jnp.float32)
    for places, weight in ((1, 8.0), (-1, -8.0), (2, -1.0), (-2, 1.0)):
        weights = jnp.where(ahead == places, weight, weights)
    return weights.astype(jnp.bfloat16)


def parts(cells):
    high = cells.astype(jnp.bfloat16)
    return high, (cells - high.astype(jnp.float32)).astype(jnp.bfloat16)


def second_diff(high, low, weights):
    fields, count, _ = high.shape
    cells = jnp.concatenate([high, low], axis=2).reshape(fields * count, 2 * LANES)
    return jnp.dot(cells, weights, preferred_element_type=jnp.float32)


def first_diff(high, low, weights):
    cells = jnp.concatenate([high, low], axis=1)
    cells = jnp.concatenate([cells[k] for k in range(FIELDS)], axis=1)
    return jnp.dot(weights, cells, preferred_element_type=jnp.float32)


def lanes(k):
    return slice(k * LANES, (k + 1) * LANES)


def primitives(state):
    density, mom_x, mom_y, mom_z, energy = state
    inverse = 1.0 / density
    vel_x, vel_y, vel_z = mom_x * inverse, mom_y * inverse, mom_z * inverse
    half = 0.5 * (vel_x * vel_x + vel_y * vel_y + vel_z * vel_z)
    press = 0.4 * (energy - density * half)
    total = energy + press
    return vel_x, vel_y, vel_z, total * inverse, half, press, total


def together(works):
    done = object()
    while works:
        works = [work for work in works if next(work, done) is not done]


def tiles(start, stop):
    return [slice(place, place + SUB) for place in range(start, stop, SUB)]


def within(cells, rows, edge, span, k):
    if edge <= rows.start and rows.stop <= span - edge:
        return cells
    place = rows.start + lax.broadcasted_iota(jnp.int32, cells.shape, 0)
    return jnp.where(jnp.logical_and(place >= edge, place < span - edge), cells, STILL[k])


def state_stage(stage, moment, base_ref, coef_ref, now_ref, flux_ref, slope_ref, lefts, weights, span):
    here, there = STATE_EDGES[moment][stage], STATE_EDGES[moment][min(stage + 1, 3)]
    for rows in tiles(here, span - here):
        source_ref = base_ref if stage == 0 else now_ref
        state = [source_ref[moment, k, rows] for k in range(FIELDS)]
        vel_x, vel_y, vel_z, heat, half, press, total = primitives(state)
        for k, cells in enumerate((vel_x, vel_y, vel_z, heat, half)):
            coef_ref[moment, stage, k, rows] = cells
        if stage == 3:
            continue
        _, mom_x, mom_y, mom_z, _ = state
        cross = mom_x * vel_y
        first = (mom_x, mom_x * vel_x + press, cross, mom_z * vel_x, total * vel_x)
        second = (mom_y, cross, mom_y * vel_y + press, mom_z * vel_y, total * vel_y)
        for k in range(FIELDS):
            flux_ref[moment, k, rows] = first[k]
            if there <= rows.start < span - there:
                slope_ref[moment, k, rows] = second[k]
    if stage == 3:
        return
    count, total_rows = span - 2 * there, span - 2 * here
    left = lefts[count, total_rows]
    flux = flux_ref[moment, :, here : span - here]
    first = first_diff(*parts(flux), left)
    slope = slope_ref[moment, :, there : span - there]
    second = second_diff(*parts(slope), weights)
    second = second.reshape(FIELDS, count, LANES)
    yield
    scale = (0.5 if stage < 2 else 1.0) * twelfth
    for k in range(FIELDS):
        for rows in tiles(there, span - there):
            local_rows = slice(rows.start - there, rows.stop - there)
            slope = first[local_rows, lanes(k)] + second[k, local_rows]
            cells = base_ref[moment, k, rows] - scale * slope
            now_ref[moment, k, rows] = within(cells, rows, BASE_RIM - STATE_RIMS[moment] + 2 * (stage + 1), span, k)


def pull_differences(moment, stage, one, adj_ref, hold_ref, first_ref, second_ref, lefts, weights):
    tall = adj_ref.shape[2]
    start = (STEPS - 1 - moment) * SUB
    edge = start + SUB if stage == 0 else start
    source_ref = adj_ref if stage == 3 else hold_ref.at[2 - stage]
    total = tall - 2 * start
    high, low = parts(source_ref[one, :, start : tall - start])
    second = second_diff(high, low, weights).reshape(FIELDS, total, LANES)
    yield True
    first = first_diff(high, low, lefts[tall - 2 * edge, total])
    yield False
    for k in range(FIELDS):
        second_ref[one, k, start : tall - start] = second[k]
        yield True
        first_ref[one, edge : tall - edge, lanes(k)] = first[:, lanes(k)]
        yield True


def pull_stage(moment, stage, one, coef_ref, adj_ref, hold_ref, first_ref, second_ref, out_ref):
    tall = adj_ref.shape[2]
    shift, last = BASE_RIM - RIM, moment == 0
    start = (STEPS - 1 - moment) * SUB
    edge = start + SUB if stage == 0 else start
    for rows in tiles(edge, tall - edge):
        base_rows = slice(rows.start + shift, rows.stop + shift)
        vel_x, vel_y, vel_z, heat, half = [coef_ref[moment, stage, k, base_rows] for k in range(5)]
        a = [first_ref[one, rows, lanes(k)] for k in range(FIELDS)]
        b = [second_ref[one, k, rows] for k in range(FIELDS)]
        mix_x = vel_x * a[1] + vel_y * a[2] + vel_z * a[3] + heat * a[4]
        mix_y = vel_x * b[1] + vel_y * b[2] + vel_z * b[3] + heat * b[4]
        lift = vel_x * a[4] + vel_y * b[4]
        press = 0.4 * (a[1] + b[2] + lift)
        term = (
            half * press - vel_x * mix_x - vel_y * mix_y,
            a[0] + mix_x + vel_x * (a[1] - press) + vel_y * b[1],
            b[0] + mix_y + vel_y * (b[2] - press) + vel_x * a[2],
            vel_x * a[3] + vel_y * b[3] - vel_z * press,
            lift + press,
        )
        for k in range(FIELDS):
            adj = adj_ref[one, k, rows]
            if stage > 0:
                scale = (1.0 if stage == 1 else 0.5) * twelfth
                hold_ref[3 - stage, one, k, rows] = adj + scale * term[k]
                continue
            one_third, two_thirds, rest = [hold_ref[place, one, k, rows] for place in range(3)]
            mean = (one_third - adj + rest + 2.0 * two_thirds) * (1.0 / 3.0)
            result = mean + (twelfth / 6.0) * term[k]
            if last:
                out_ref[one, k, rows.start - RIM : rows.stop - RIM] = result
            else:
                adj_ref[one, k, rows] = result
        yield


def kernel(
    seeds_ref, near_ref, far_ref, blocks_ref, out_ref,
    adj_ref, hold_ref, first_ref, second_ref,
    base_ref, coef_ref, now_ref, flux_ref, slope_ref,
):
    funcs, _, strip, _ = seeds_ref.shape
    spread, _, block, _ = blocks_ref.shape
    tall, span = strip + 2 * RIM, strip + 2 * BASE_RIM
    even = lax.rem(lax.axis_index("tile"), 2) == 0

    def lay(left_ref, right_ref):
        for one in range(funcs):
            for k in range(FIELDS):
                adj_ref[one, k, :RIM] = left_ref[one, k]
                adj_ref[one, k, RIM + strip :] = right_ref[one, k]

    def lay_base(part, moment, shift, low, high):
        for owner in range(spread):
            start, stop = max(low, owner * block), min(high, (owner + 1) * block)
            if start < stop:
                rows = slice(start - owner * block, stop - owner * block)
                place = BASE_RIM + shift + start
                for k in range(FIELDS):
                    base_ref[moment, k, place : place + stop - start, :] = blocks_ref[owner, part * FIELDS + k, rows, :]

    for moment in range(STEPS):
        edge = BASE_RIM - STATE_RIMS[moment]
        for start in (STATE_EDGES[moment][0], span - STATE_EDGES[moment][0] - SUB):
            if start < edge or start + SUB > span - edge:
                for k in range(FIELDS):
                    base_ref[moment, k, start : start + SUB] = jnp.full((SUB, LANES), STILL[k], jnp.float32)
    middle = strip // 2
    lay_base(0, 0, 0, 0, strip)
    lay_base(1, 1, 0, 0, strip)
    lay_base(2, 1, strip, 0, middle)
    lay_base(2, 1, -strip, middle, strip)
    lay_base(3, 0, strip, 0, SHORT_RIM)
    lay_base(3, 1, -strip, max(SHORT_RIM, strip - LONG_RIM), middle)
    lay_base(3, 1, strip, middle, min(LONG_RIM, strip - SHORT_RIM))
    lay_base(3, 0, -strip, strip - SHORT_RIM, strip)

    weights = second_weights()
    sizes = {(tall - 2 * start, tall - 2 * start) for start in range(0, STEPS * SUB, SUB)}
    sizes |= {(tall - 2 * start - 2 * SUB, tall - 2 * start) for start in range(0, STEPS * SUB, SUB)}
    for edges in STATE_EDGES:
        sizes |= {(span - 2 * edges[n + 1], span - 2 * edges[n]) for n in range(3)}
    lefts = {size: first_weights(*size, (size[1] - size[0]) // 2) for size in sorted(sizes)}
    def states(moment):
        for stage in range(4):
            yield from state_stage(
                stage, moment, base_ref, coef_ref, now_ref, flux_ref, slope_ref, lefts, weights, span
            )

    def differences(moment, stage, one):
        return pull_differences(moment, stage, one, adj_ref, hold_ref, first_ref, second_ref, lefts, weights)

    pl.when(even)(lambda: lay(far_ref, near_ref))
    pl.when(jnp.logical_not(even))(lambda: lay(near_ref, far_ref))
    for one in range(funcs):
        for k in range(FIELDS):
            adj_ref[one, k, RIM : RIM + strip] = seeds_ref[one, k]
    together([chain(*(differences(STEPS - 1, 3, one) for one in range(funcs))), states(1), states(0)])
    starting, storing = iter(()), iter(())
    for moment in reversed(range(STEPS)):
        for stage in (3, 2, 1, 0):
            for one in range(funcs):
                work = pull_stage(moment, stage, one, coef_ref, adj_ref, hold_ref, first_ref, second_ref, out_ref)
                begun = False
                for number, _ in enumerate(work):
                    if number % START_EVERY == 0 and not begun:
                        begun = next(starting, False) is False
                    for _ in range(STORES):
                        next(storing, None)
                while not begun:
                    begun = next(starting, False) is False
                for _ in storing:
                    pass
                storing, starting = starting, iter(())
                if stage > 0:
                    starting = differences(moment, stage - 1, one)
                elif moment > 0:
                    starting = differences(moment - 1, 3, one)


def local(seeds, checkpoints):
    funcs, _, strip, _ = seeds.shape
    block = checkpoints.shape[2]
    even = lax.rem(lax.axis_index("tile"), 2) == 0
    far_base, near_base = swap_far(checkpoints), swap_near(checkpoints)
    tail = strip - RIM
    far_edge = lax.dynamic_slice_in_dim(seeds, jnp.where(even, 0, tail), RIM, axis=2)
    near_edge = lax.dynamic_slice_in_dim(seeds, jnp.where(even, tail, 0), RIM, axis=2)
    own = checkpoints.reshape(STEPS * FIELDS, block, LANES)
    roomy = jnp.pad(own, ((0, STEPS * FIELDS), (0, 0), (0, 0)))
    roomy, far_edge, near_edge = lax.optimization_barrier((roomy, far_edge, near_edge))
    far, near = swap_far(far_edge), swap_near(near_edge)
    lower = lax.axis_index("func") * block < strip // 2
    take_far = even != lower
    main = lax.select(take_far, far_base, near_base)
    other = lax.select(take_far, near_base[1], far_base[1])
    place = lax.axis_index("func") * block + lax.broadcasted_iota(jnp.int32, (1, block, 1), 1)
    inner = jnp.logical_and(place >= SHORT_RIM, place < strip - SHORT_RIM)
    rest = jnp.where(inner, other, main[0])
    packed = lax.dynamic_update_slice(roomy, jnp.concatenate([main[1], rest], axis=0), (STEPS * FIELDS, 0, 0))
    blocks = lax.all_gather(packed, "func", axis=0, tiled=False)
    tall, span = strip + 2 * RIM, strip + 2 * BASE_RIM
    shapes = [
        (funcs, FIELDS, tall, LANES),
        (3, funcs, FIELDS, tall, LANES),
        (funcs, tall, FIELDS * LANES),
        (funcs, FIELDS, tall, LANES),
        (STEPS, FIELDS, span, LANES),
        (STEPS, 4, 5, span, LANES),
        (STEPS, FIELDS, span, LANES),
        (STEPS, FIELDS, span, LANES),
        (STEPS, FIELDS, span, LANES),
    ]
    vmem = pl.BlockSpec(memory_space=pltpu.VMEM)
    return pl.pallas_call(
        kernel,
        out_shape=jax.ShapeDtypeStruct(seeds.shape, jnp.float32),
        in_specs=[vmem] * 4,
        out_specs=vmem,
        scratch_shapes=[pltpu.VMEM(shape, jnp.float32) for shape in shapes],
        compiler_params=pltpu.CompilerParams(vmem_limit_bytes=32 * 1024 * 1024),
        name="two_steps",
    )(seeds, near, far, blocks)


def solution(mesh):
    return jax.shard_map(
        local,
        mesh=mesh,
        in_specs=(P("func", None, "tile", None), P(None, None, ("tile", "func"), None)),
        out_specs=P("func", None, "tile", None),
        check_vma=False,
    )
```

```python
from itertools import chain

import jax
import jax.numpy as jnp
from jax import lax
from jax.experimental import pallas as pl
from jax.experimental.pallas import tpu as pltpu
from jax.sharding import PartitionSpec as P

NZ = 4
STEPS = 2
FIELDS = 5
LANES = 128
SUB = 8

step_size = 0.3
twelfth = step_size / 12.0

RIM = 16
BASE_RIM = 24
LONG_RIM = 20
SHORT_RIM = 12
STATE_RIMS = (SHORT_RIM, LONG_RIM)
START_EVERY, STORES = 2, 2
STILL = (1.0, 0.0, 0.0, 0.0, 2.5)
STATE_EDGES = ((8, 8, 16, 16), (0, 0, 8, 8))


def swap_near(cells):
    count = lax.axis_size("tile")
    return lax.ppermute(cells, "tile", [(i, i ^ 1) for i in range(count)])


def swap_far(cells):
    count = lax.axis_size("tile")
    pairs = [(i, (i + (1 if i % 2 else -1)) % count) for i in range(count)]
    return lax.ppermute(cells, "tile", pairs)


def second_weights():
    shape = (LANES, LANES)
    ahead = lax.broadcasted_iota(jnp.int32, shape, 0) - lax.broadcasted_iota(jnp.int32, shape, 1)
    ahead = jnp.bitwise_and(ahead, LANES - 1)
    weights = jnp.zeros(shape, jnp.float32)
    for places, weight in ((NZ, 8.0), (-NZ, -8.0), (2 * NZ, -1.0), (-2 * NZ, 1.0)):
        weights = jnp.where(ahead == places % LANES, weight, weights)
    return jnp.concatenate([weights, weights], axis=0).astype(jnp.bfloat16)


def first_weights(count, total, skip):
    shape = (count, 2 * total)
    column = lax.broadcasted_iota(jnp.int32, shape, 1)
    column = jnp.where(column < total, column, column - total)
    ahead = column - lax.broadcasted_iota(jnp.int32, shape, 0) - skip
    weights = jnp.zeros(shape, jnp.float32)
    for places, weight in ((1, 8.0), (-1, -8.0), (2, -1.0), (-2, 1.0)):
        weights = jnp.where(ahead == places, weight, weights)
    return weights.astype(jnp.bfloat16)


def parts(cells):
    high = cells.astype(jnp.bfloat16)
    return high, (cells - high.astype(jnp.float32)).astype(jnp.bfloat16)


def second_diff(high, low, weights):
    fields, count, _ = high.shape
    cells = jnp.concatenate([high, low], axis=2).reshape(fields * count, 2 * LANES)
    return jnp.dot(cells, weights, preferred_element_type=jnp.float32)


def first_diff(high, low, weights):
    cells = jnp.concatenate([high, low], axis=1)
    cells = jnp.concatenate([cells[k] for k in range(FIELDS)], axis=1)
    return jnp.dot(weights, cells, preferred_element_type=jnp.float32)


def lanes(k):
    return slice(k * LANES, (k + 1) * LANES)


def primitives(state):
    density, mom_x, mom_y, mom_z, energy = state
    inverse = 1.0 / density
    vel_x, vel_y, vel_z = mom_x * inverse, mom_y * inverse, mom_z * inverse
    half = 0.5 * (vel_x * vel_x + vel_y * vel_y + vel_z * vel_z)
    press = 0.4 * (energy - density * half)
    total = energy + press
    return vel_x, vel_y, vel_z, total * inverse, half, press, total


def together(works):
    done = object()
    while works:
        works = [work for work in works if next(work, done) is not done]


def tiles(start, stop):
    return [slice(place, place + SUB) for place in range(start, stop, SUB)]


def within(cells, rows, edge, span, k):
    if edge <= rows.start and rows.stop <= span - edge:
        return cells
    place = rows.start + lax.broadcasted_iota(jnp.int32, cells.shape, 0)
    return jnp.where(jnp.logical_and(place >= edge, place < span - edge), cells, STILL[k])


def state_stage(stage, moment, base_ref, coef_ref, now_ref, flux_ref, slope_ref, lefts, weights, span):
    here, there = STATE_EDGES[moment][stage], STATE_EDGES[moment][min(stage + 1, 3)]
    for rows in tiles(here, span - here):
        source_ref = base_ref if stage == 0 else now_ref
        state = [source_ref[moment, k, rows] for k in range(FIELDS)]
        vel_x, vel_y, vel_z, heat, half, press, total = primitives(state)
        for k, cells in enumerate((vel_x, vel_y, vel_z, heat, half)):
            coef_ref[moment, stage, k, rows] = cells
        if stage == 3:
            continue
        _, mom_x, mom_y, mom_z, _ = state
        cross = mom_x * vel_y
        first = (mom_x, mom_x * vel_x + press, cross, mom_z * vel_x, total * vel_x)
        second = (mom_y, cross, mom_y * vel_y + press, mom_z * vel_y, total * vel_y)
        for k in range(FIELDS):
            flux_ref[moment, k, rows] = first[k]
            if there <= rows.start < span - there:
                slope_ref[moment, k, rows] = second[k]
    if stage == 3:
        return
    count, total_rows = span - 2 * there, span - 2 * here
    left = lefts[count, total_rows]
    flux = flux_ref[moment, :, here : span - here]
    first = first_diff(*parts(flux), left)
    slope = slope_ref[moment, :, there : span - there]
    second = second_diff(*parts(slope), weights)
    second = second.reshape(FIELDS, count, LANES)
    yield
    scale = (0.5 if stage < 2 else 1.0) * twelfth
    for k in range(FIELDS):
        for rows in tiles(there, span - there):
            local_rows = slice(rows.start - there, rows.stop - there)
            slope = first[local_rows, lanes(k)] + second[k, local_rows]
            cells = base_ref[moment, k, rows] - scale * slope
            now_ref[moment, k, rows] = within(cells, rows, BASE_RIM - STATE_RIMS[moment] + 2 * (stage + 1), span, k)


def pull_differences(moment, stage, one, adj_ref, hold_ref, first_ref, second_ref, lefts, weights):
    tall = adj_ref.shape[2]
    start = (STEPS - 1 - moment) * SUB
    edge = start + SUB if stage == 0 else start
    source_ref = adj_ref if stage == 3 else hold_ref.at[2 - stage]
    total = tall - 2 * start
    high, low = parts(source_ref[one, :, start : tall - start])
    second = second_diff(high, low, weights).reshape(FIELDS, total, LANES)
    yield True
    first = first_diff(high, low, lefts[tall - 2 * edge, total])
    yield False
    for k in range(FIELDS):
        second_ref[one, k, start : tall - start] = second[k]
        yield True
        first_ref[one, edge : tall - edge, lanes(k)] = first[:, lanes(k)]
        yield True


def pull_stage(moment, stage, one, coef_ref, adj_ref, hold_ref, first_ref, second_ref, out_ref):
    tall = adj_ref.shape[2]
    shift, last = BASE_RIM - RIM, moment == 0
    start = (STEPS - 1 - moment) * SUB
    edge = start + SUB if stage == 0 else start
    for rows in tiles(edge, tall - edge):
        base_rows = slice(rows.start + shift, rows.stop + shift)
        vel_x, vel_y, vel_z, heat, half = [coef_ref[moment, stage, k, base_rows] for k in range(5)]
        a = [first_ref[one, rows, lanes(k)] for k in range(FIELDS)]
        b = [second_ref[one, k, rows] for k in range(FIELDS)]
        mix_x = vel_x * a[1] + vel_y * a[2] + vel_z * a[3] + heat * a[4]
        mix_y = vel_x * b[1] + vel_y * b[2] + vel_z * b[3] + heat * b[4]
        lift = vel_x * a[4] + vel_y * b[4]
        press = 0.4 * (a[1] + b[2] + lift)
        term = (
            half * press - vel_x * mix_x - vel_y * mix_y,
            a[0] + mix_x + vel_x * (a[1] - press) + vel_y * b[1],
            b[0] + mix_y + vel_y * (b[2] - press) + vel_x * a[2],
            vel_x * a[3] + vel_y * b[3] - vel_z * press,
            lift + press,
        )
        for k in range(FIELDS):
            adj = adj_ref[one, k, rows]
            if stage > 0:
                scale = (1.0 if stage == 1 else 0.5) * twelfth
                hold_ref[3 - stage, one, k, rows] = adj + scale * term[k]
                continue
            one_third, two_thirds, rest = [hold_ref[place, one, k, rows] for place in range(3)]
            mean = (one_third - adj + rest + 2.0 * two_thirds) * (1.0 / 3.0)
            result = mean + (twelfth / 6.0) * term[k]
            if last:
                out_ref[one, k, rows.start - RIM : rows.stop - RIM] = result
            else:
                adj_ref[one, k, rows] = result
        yield


def kernel(
    seeds_ref, far_ref, near_ref, blocks_ref, out_ref,
    adj_ref, hold_ref, first_ref, second_ref,
    base_ref, coef_ref, now_ref, flux_ref, slope_ref,
):
    funcs, _, strip, _ = seeds_ref.shape
    spread, _, block, _ = blocks_ref.shape
    tall, span = strip + 2 * RIM, strip + 2 * BASE_RIM
    even = lax.rem(lax.axis_index("tile"), 2) == 0

    def lay(left_ref, right_ref):
        for one in range(funcs):
            for k in range(FIELDS):
                adj_ref[one, k, :RIM] = left_ref[one, k]
                adj_ref[one, k, RIM + strip :] = right_ref[one, k]

    def lay_base(part, moment, shift, low, high):
        for owner in range(spread):
            start, stop = max(low, owner * block), min(high, (owner + 1) * block)
            if start < stop:
                rows = slice(start - owner * block, stop - owner * block)
                place = BASE_RIM + shift + start
                for k in range(FIELDS):
                    base_ref[moment, k, place : place + stop - start, :] = blocks_ref[owner, part * FIELDS + k, rows, :]

    for moment in range(STEPS):
        edge = BASE_RIM - STATE_RIMS[moment]
        for start in (STATE_EDGES[moment][0], span - STATE_EDGES[moment][0] - SUB):
            if start < edge or start + SUB > span - edge:
                for k in range(FIELDS):
                    base_ref[moment, k, start : start + SUB] = jnp.full((SUB, LANES), STILL[k], jnp.float32)
    middle = strip // 2
    lay_base(0, 0, 0, 0, strip)
    lay_base(1, 1, 0, 0, strip)
    lay_base(2, 1, strip, 0, middle)
    lay_base(2, 1, -strip, middle, strip)
    lay_base(3, 0, strip, 0, SHORT_RIM)
    lay_base(3, 1, -strip, max(SHORT_RIM, strip - LONG_RIM), middle)
    lay_base(3, 1, strip, middle, min(LONG_RIM, strip - SHORT_RIM))
    lay_base(3, 0, -strip, strip - SHORT_RIM, strip)

    weights = second_weights()
    sizes = {(tall - 2 * start, tall - 2 * start) for start in range(0, STEPS * SUB, SUB)}
    sizes |= {(tall - 2 * start - 2 * SUB, tall - 2 * start) for start in range(0, STEPS * SUB, SUB)}
    for edges in STATE_EDGES:
        sizes |= {(span - 2 * edges[n + 1], span - 2 * edges[n]) for n in range(3)}
    lefts = {size: first_weights(*size, (size[1] - size[0]) // 2) for size in sorted(sizes)}
    def states(moment):
        for stage in range(4):
            yield from state_stage(
                stage, moment, base_ref, coef_ref, now_ref, flux_ref, slope_ref, lefts, weights, span
            )

    def differences(moment, stage, one):
        return pull_differences(moment, stage, one, adj_ref, hold_ref, first_ref, second_ref, lefts, weights)

    pl.when(even)(lambda: lay(far_ref, near_ref))
    pl.when(jnp.logical_not(even))(lambda: lay(near_ref, far_ref))
    for one in range(funcs):
        for k in range(FIELDS):
            adj_ref[one, k, RIM : RIM + strip] = seeds_ref[one, k]
    together([chain(*(differences(STEPS - 1, 3, one) for one in range(funcs))), states(1), states(0)])
    starting, storing = iter(()), iter(())
    for moment in reversed(range(STEPS)):
        for stage in (3, 2, 1, 0):
            for one in range(funcs):
                work = pull_stage(moment, stage, one, coef_ref, adj_ref, hold_ref, first_ref, second_ref, out_ref)
                begun = False
                for number, _ in enumerate(work):
                    if number % START_EVERY == 0 and not begun:
                        begun = next(starting, False) is False
                    for _ in range(STORES):
                        next(storing, None)
                while not begun:
                    begun = next(starting, False) is False
                for _ in storing:
                    pass
                storing, starting = starting, iter(())
                if stage > 0:
                    starting = differences(moment, stage - 1, one)
                elif moment > 0:
                    starting = differences(moment - 1, 3, one)


def local(seeds, checkpoints):
    funcs, _, strip, _ = seeds.shape
    block = checkpoints.shape[2]
    even = lax.rem(lax.axis_index("tile"), 2) == 0
    far_base, near_base = swap_far(checkpoints), swap_near(checkpoints)
    tail = strip - RIM
    far_edge = lax.dynamic_slice_in_dim(seeds, jnp.where(even, 0, tail), RIM, axis=2)
    near_edge = lax.dynamic_slice_in_dim(seeds, jnp.where(even, tail, 0), RIM, axis=2)
    own = checkpoints.reshape(STEPS * FIELDS, block, LANES)
    roomy = jnp.pad(own, ((0, STEPS * FIELDS), (0, 0), (0, 0)))
    roomy, far_base = lax.optimization_barrier((roomy, far_base))
    far, near = swap_far(far_edge), swap_near(near_edge)
    lower = lax.axis_index("func") * block < strip // 2
    take_far = even != lower
    main = lax.select(take_far, far_base, near_base)
    other = lax.select(take_far, near_base[1], far_base[1])
    place = lax.axis_index("func") * block + lax.broadcasted_iota(jnp.int32, (1, block, 1), 1)
    inner = jnp.logical_and(place >= SHORT_RIM, place < strip - SHORT_RIM)
    rest = jnp.where(inner, other, main[0])
    packed = lax.dynamic_update_slice(roomy, jnp.concatenate([main[1], rest], axis=0), (STEPS * FIELDS, 0, 0))
    blocks = lax.all_gather(packed, "func", axis=0, tiled=False)
    tall, span = strip + 2 * RIM, strip + 2 * BASE_RIM
    shapes = [
        (funcs, FIELDS, tall, LANES),
        (3, funcs, FIELDS, tall, LANES),
        (funcs, tall, FIELDS * LANES),
        (funcs, FIELDS, tall, LANES),
        (STEPS, FIELDS, span, LANES),
        (STEPS, 4, 5, span, LANES),
        (STEPS, FIELDS, span, LANES),
        (STEPS, FIELDS, span, LANES),
        (STEPS, FIELDS, span, LANES),
    ]
    vmem = pl.BlockSpec(memory_space=pltpu.VMEM)
    return pl.pallas_call(
        kernel,
        out_shape=jax.ShapeDtypeStruct(seeds.shape, jnp.float32),
        in_specs=[vmem] * 4,
        out_specs=vmem,
        scratch_shapes=[pltpu.VMEM(shape, jnp.float32) for shape in shapes],
        compiler_params=pltpu.CompilerParams(vmem_limit_bytes=32 * 1024 * 1024),
        name="two_steps",
    )(seeds, far, near, blocks)


def solution(mesh):
    return jax.shard_map(
        local,
        mesh=mesh,
        in_specs=(P("func", None, "tile", None), P(None, None, ("tile", "func"), None)),
        out_specs=P("func", None, "tile", None),
        check_vma=False,
    )
```

```python
from itertools import chain

import jax
import jax.numpy as jnp
from jax import lax
from jax.experimental import pallas as pl
from jax.experimental.pallas import tpu as pltpu
from jax.sharding import PartitionSpec as P

NZ = 4
STEPS = 2
FIELDS = 5
LANES = 128
SUB = 8

step_size = 0.3
twelfth = step_size / 12.0

RIM = 16
BASE_RIM = 24
LONG_RIM = 20
SHORT_RIM = 12
STATE_RIMS = (SHORT_RIM, LONG_RIM)
START_EVERY, STORES = 2, 2
STILL = (1.0, 0.0, 0.0, 0.0, 2.5)
STATE_EDGES = ((8, 8, 16, 16), (0, 0, 8, 8))


def swap_near(cells):
    count = lax.axis_size("tile")
    return lax.ppermute(cells, "tile", [(i, i ^ 1) for i in range(count)])


def shift(cells, places):
    count = lax.axis_size("tile")
    return lax.ppermute(cells, "tile", [(i, (i + places) % count) for i in range(count)])


def swap_far(cells):
    count = lax.axis_size("tile")
    pairs = [(i, (i + (1 if i % 2 else -1)) % count) for i in range(count)]
    return lax.ppermute(cells, "tile", pairs)


def second_weights():
    shape = (LANES, LANES)
    ahead = lax.broadcasted_iota(jnp.int32, shape, 0) - lax.broadcasted_iota(jnp.int32, shape, 1)
    ahead = jnp.bitwise_and(ahead, LANES - 1)
    weights = jnp.zeros(shape, jnp.float32)
    for places, weight in ((NZ, 8.0), (-NZ, -8.0), (2 * NZ, -1.0), (-2 * NZ, 1.0)):
        weights = jnp.where(ahead == places % LANES, weight, weights)
    return jnp.concatenate([weights, weights], axis=0).astype(jnp.bfloat16)


def first_weights(count, total, skip):
    shape = (count, 2 * total)
    column = lax.broadcasted_iota(jnp.int32, shape, 1)
    column = jnp.where(column < total, column, column - total)
    ahead = column - lax.broadcasted_iota(jnp.int32, shape, 0) - skip
    weights = jnp.zeros(shape, jnp.float32)
    for places, weight in ((1, 8.0), (-1, -8.0), (2, -1.0), (-2, 1.0)):
        weights = jnp.where(ahead == places, weight, weights)
    return weights.astype(jnp.bfloat16)


def parts(cells):
    high = cells.astype(jnp.bfloat16)
    return high, (cells - high.astype(jnp.float32)).astype(jnp.bfloat16)


def second_diff(high, low, weights):
    fields, count, _ = high.shape
    cells = jnp.concatenate([high, low], axis=2).reshape(fields * count, 2 * LANES)
    return jnp.dot(cells, weights, preferred_element_type=jnp.float32)


def first_diff(high, low, weights):
    cells = jnp.concatenate([high, low], axis=1)
    cells = jnp.concatenate([cells[k] for k in range(FIELDS)], axis=1)
    return jnp.dot(weights, cells, preferred_element_type=jnp.float32)


def lanes(k):
    return slice(k * LANES, (k + 1) * LANES)


def primitives(state):
    density, mom_x, mom_y, mom_z, energy = state
    inverse = 1.0 / density
    vel_x, vel_y, vel_z = mom_x * inverse, mom_y * inverse, mom_z * inverse
    half = 0.5 * (vel_x * vel_x + vel_y * vel_y + vel_z * vel_z)
    press = 0.4 * (energy - density * half)
    total = energy + press
    return vel_x, vel_y, vel_z, total * inverse, half, press, total


def together(works):
    done = object()
    while works:
        works = [work for work in works if next(work, done) is not done]


def tiles(start, stop):
    return [slice(place, place + SUB) for place in range(start, stop, SUB)]


def within(cells, rows, edge, span, k):
    if edge <= rows.start and rows.stop <= span - edge:
        return cells
    place = rows.start + lax.broadcasted_iota(jnp.int32, cells.shape, 0)
    return jnp.where(jnp.logical_and(place >= edge, place < span - edge), cells, STILL[k])


def state_stage(stage, moment, base_ref, coef_ref, now_ref, flux_ref, slope_ref, lefts, weights, span):
    here, there = STATE_EDGES[moment][stage], STATE_EDGES[moment][min(stage + 1, 3)]
    for rows in tiles(here, span - here):
        source_ref = base_ref if stage == 0 else now_ref
        state = [source_ref[moment, k, rows] for k in range(FIELDS)]
        vel_x, vel_y, vel_z, heat, half, press, total = primitives(state)
        for k, cells in enumerate((vel_x, vel_y, vel_z, heat, half)):
            coef_ref[moment, stage, k, rows] = cells
        if stage == 3:
            continue
        _, mom_x, mom_y, mom_z, _ = state
        cross = mom_x * vel_y
        first = (mom_x, mom_x * vel_x + press, cross, mom_z * vel_x, total * vel_x)
        second = (mom_y, cross, mom_y * vel_y + press, mom_z * vel_y, total * vel_y)
        for k in range(FIELDS):
            flux_ref[moment, k, rows] = first[k]
            if there <= rows.start < span - there:
                slope_ref[moment, k, rows] = second[k]
    if stage == 3:
        return
    count, total_rows = span - 2 * there, span - 2 * here
    left = lefts[count, total_rows]
    flux = flux_ref[moment, :, here : span - here]
    first = first_diff(*parts(flux), left)
    slope = slope_ref[moment, :, there : span - there]
    second = second_diff(*parts(slope), weights)
    second = second.reshape(FIELDS, count, LANES)
    yield
    scale = (0.5 if stage < 2 else 1.0) * twelfth
    for k in range(FIELDS):
        for rows in tiles(there, span - there):
            local_rows = slice(rows.start - there, rows.stop - there)
            slope = first[local_rows, lanes(k)] + second[k, local_rows]
            cells = base_ref[moment, k, rows] - scale * slope
            now_ref[moment, k, rows] = within(cells, rows, BASE_RIM - STATE_RIMS[moment] + 2 * (stage + 1), span, k)


def pull_differences(moment, stage, one, adj_ref, hold_ref, first_ref, second_ref, lefts, weights):
    tall = adj_ref.shape[2]
    start = (STEPS - 1 - moment) * SUB
    edge = start + SUB if stage == 0 else start
    source_ref = adj_ref if stage == 3 else hold_ref.at[2 - stage]
    total = tall - 2 * start
    high, low = parts(source_ref[one, :, start : tall - start])
    second = second_diff(high, low, weights).reshape(FIELDS, total, LANES)
    yield True
    first = first_diff(high, low, lefts[tall - 2 * edge, total])
    yield False
    for k in range(FIELDS):
        second_ref[one, k, start : tall - start] = second[k]
        yield True
        first_ref[one, edge : tall - edge, lanes(k)] = first[:, lanes(k)]
        yield True


def pull_stage(moment, stage, one, coef_ref, adj_ref, hold_ref, first_ref, second_ref, out_ref):
    tall = adj_ref.shape[2]
    shift, last = BASE_RIM - RIM, moment == 0
    start = (STEPS - 1 - moment) * SUB
    edge = start + SUB if stage == 0 else start
    for rows in tiles(edge, tall - edge):
        base_rows = slice(rows.start + shift, rows.stop + shift)
        vel_x, vel_y, vel_z, heat, half = [coef_ref[moment, stage, k, base_rows] for k in range(5)]
        a = [first_ref[one, rows, lanes(k)] for k in range(FIELDS)]
        b = [second_ref[one, k, rows] for k in range(FIELDS)]
        mix_x = vel_x * a[1] + vel_y * a[2] + vel_z * a[3] + heat * a[4]
        mix_y = vel_x * b[1] + vel_y * b[2] + vel_z * b[3] + heat * b[4]
        lift = vel_x * a[4] + vel_y * b[4]
        press = 0.4 * (a[1] + b[2] + lift)
        term = (
            half * press - vel_x * mix_x - vel_y * mix_y,
            a[0] + mix_x + vel_x * (a[1] - press) + vel_y * b[1],
            b[0] + mix_y + vel_y * (b[2] - press) + vel_x * a[2],
            vel_x * a[3] + vel_y * b[3] - vel_z * press,
            lift + press,
        )
        for k in range(FIELDS):
            adj = adj_ref[one, k, rows]
            if stage > 0:
                scale = (1.0 if stage == 1 else 0.5) * twelfth
                hold_ref[3 - stage, one, k, rows] = adj + scale * term[k]
                continue
            one_third, two_thirds, rest = [hold_ref[place, one, k, rows] for place in range(3)]
            mean = (one_third - adj + rest + 2.0 * two_thirds) * (1.0 / 3.0)
            result = mean + (twelfth / 6.0) * term[k]
            if last:
                out_ref[one, k, rows.start - RIM : rows.stop - RIM] = result
            else:
                adj_ref[one, k, rows] = result
        yield


def kernel(
    seeds_ref, near_ref, far_ref, blocks_ref, out_ref,
    adj_ref, hold_ref, first_ref, second_ref,
    base_ref, coef_ref, now_ref, flux_ref, slope_ref,
):
    funcs, _, strip, _ = seeds_ref.shape
    spread, _, block, _ = blocks_ref.shape
    tall, span = strip + 2 * RIM, strip + 2 * BASE_RIM
    even = lax.rem(lax.axis_index("tile"), 2) == 0

    def lay(left_ref, right_ref):
        for one in range(funcs):
            for k in range(FIELDS):
                adj_ref[one, k, :RIM] = left_ref[one, k]
                adj_ref[one, k, RIM + strip :] = right_ref[one, k]

    def lay_base(part, moment, shift, low, high):
        for owner in range(spread):
            start, stop = max(low, owner * block), min(high, (owner + 1) * block)
            if start < stop:
                rows = slice(start - owner * block, stop - owner * block)
                place = BASE_RIM + shift + start
                for k in range(FIELDS):
                    base_ref[moment, k, place : place + stop - start, :] = blocks_ref[owner, part * FIELDS + k, rows, :]

    for moment in range(STEPS):
        edge = BASE_RIM - STATE_RIMS[moment]
        for start in (STATE_EDGES[moment][0], span - STATE_EDGES[moment][0] - SUB):
            if start < edge or start + SUB > span - edge:
                for k in range(FIELDS):
                    base_ref[moment, k, start : start + SUB] = jnp.full((SUB, LANES), STILL[k], jnp.float32)
    middle = strip // 2
    lay_base(0, 0, 0, 0, strip)
    lay_base(1, 1, 0, 0, strip)
    lay_base(2, 1, strip, 0, middle)
    lay_base(2, 1, -strip, middle, strip)
    lay_base(3, 0, strip, 0, SHORT_RIM)
    lay_base(3, 1, -strip, max(SHORT_RIM, strip - LONG_RIM), middle)
    lay_base(3, 1, strip, middle, min(LONG_RIM, strip - SHORT_RIM))
    lay_base(3, 0, -strip, strip - SHORT_RIM, strip)

    weights = second_weights()
    sizes = {(tall - 2 * start, tall - 2 * start) for start in range(0, STEPS * SUB, SUB)}
    sizes |= {(tall - 2 * start - 2 * SUB, tall - 2 * start) for start in range(0, STEPS * SUB, SUB)}
    for edges in STATE_EDGES:
        sizes |= {(span - 2 * edges[n + 1], span - 2 * edges[n]) for n in range(3)}
    lefts = {size: first_weights(*size, (size[1] - size[0]) // 2) for size in sorted(sizes)}
    def states(moment):
        for stage in range(4):
            yield from state_stage(
                stage, moment, base_ref, coef_ref, now_ref, flux_ref, slope_ref, lefts, weights, span
            )

    def differences(moment, stage, one):
        return pull_differences(moment, stage, one, adj_ref, hold_ref, first_ref, second_ref, lefts, weights)

    pl.when(even)(lambda: lay(far_ref, near_ref))
    pl.when(jnp.logical_not(even))(lambda: lay(near_ref, far_ref))
    for one in range(funcs):
        for k in range(FIELDS):
            adj_ref[one, k, RIM : RIM + strip] = seeds_ref[one, k]
    together([chain(*(differences(STEPS - 1, 3, one) for one in range(funcs))), states(1), states(0)])
    starting, storing = iter(()), iter(())
    for moment in reversed(range(STEPS)):
        for stage in (3, 2, 1, 0):
            for one in range(funcs):
                work = pull_stage(moment, stage, one, coef_ref, adj_ref, hold_ref, first_ref, second_ref, out_ref)
                begun = False
                for number, _ in enumerate(work):
                    if number % START_EVERY == 0 and not begun:
                        begun = next(starting, False) is False
                    for _ in range(STORES):
                        next(storing, None)
                while not begun:
                    begun = next(starting, False) is False
                for _ in storing:
                    pass
                storing, starting = starting, iter(())
                if stage > 0:
                    starting = differences(moment, stage - 1, one)
                elif moment > 0:
                    starting = differences(moment - 1, 3, one)


def local(seeds, checkpoints):
    funcs, _, strip, _ = seeds.shape
    block = checkpoints.shape[2]
    even = lax.rem(lax.axis_index("tile"), 2) == 0
    left, right = shift(checkpoints, 1), shift(checkpoints, -1)
    tail = strip - RIM
    far_edge = lax.dynamic_slice_in_dim(seeds, jnp.where(even, 0, tail), RIM, axis=2)
    near_edge = lax.dynamic_slice_in_dim(seeds, jnp.where(even, tail, 0), RIM, axis=2)
    own = checkpoints.reshape(STEPS * FIELDS, block, LANES)
    roomy = jnp.pad(own, ((0, STEPS * FIELDS), (0, 0), (0, 0)))
    roomy, right = lax.optimization_barrier((roomy, right))
    far, near = swap_far(far_edge), swap_near(near_edge)
    lower = lax.axis_index("func") * block < strip // 2
    main = lax.select(lower, right, left)
    other = lax.select(lower, left[1], right[1])
    place = lax.axis_index("func") * block + lax.broadcasted_iota(jnp.int32, (1, block, 1), 1)
    inner = jnp.logical_and(place >= SHORT_RIM, place < strip - SHORT_RIM)
    rest = jnp.where(inner, other, main[0])
    packed = lax.dynamic_update_slice(roomy, jnp.concatenate([main[1], rest], axis=0), (STEPS * FIELDS, 0, 0))
    blocks = lax.all_gather(packed, "func", axis=0, tiled=False)
    tall, span = strip + 2 * RIM, strip + 2 * BASE_RIM
    shapes = [
        (funcs, FIELDS, tall, LANES),
        (3, funcs, FIELDS, tall, LANES),
        (funcs, tall, FIELDS * LANES),
        (funcs, FIELDS, tall, LANES),
        (STEPS, FIELDS, span, LANES),
        (STEPS, 4, 5, span, LANES),
        (STEPS, FIELDS, span, LANES),
        (STEPS, FIELDS, span, LANES),
        (STEPS, FIELDS, span, LANES),
    ]
    vmem = pl.BlockSpec(memory_space=pltpu.VMEM)
    return pl.pallas_call(
        kernel,
        out_shape=jax.ShapeDtypeStruct(seeds.shape, jnp.float32),
        in_specs=[vmem] * 4,
        out_specs=vmem,
        scratch_shapes=[pltpu.VMEM(shape, jnp.float32) for shape in shapes],
        compiler_params=pltpu.CompilerParams(vmem_limit_bytes=32 * 1024 * 1024),
        name="two_steps",
    )(seeds, near, far, blocks)


def solution(mesh):
    return jax.shard_map(
        local,
        mesh=mesh,
        in_specs=(P("func", None, "tile", None), P(None, None, ("tile", "func"), None)),
        out_specs=P("func", None, "tile", None),
        check_vma=False,
    )
```

```python
from itertools import chain

import jax
import jax.numpy as jnp
import numpy as np
from jax import lax
from jax.experimental import pallas as pl
from jax.experimental.pallas import tpu as pltpu
from jax.sharding import PartitionSpec as P

NZ = 4
STEPS = 2
FIELDS = 5
LANES = 128
SUB = 8

step_size = 0.3
twelfth = step_size / 12.0

RIM = 16
BASE_RIM = 24
LONG_RIM = 20
SHORT_RIM = 12
STATE_RIMS = (SHORT_RIM, LONG_RIM)
START_EVERY, STORES = 2, 2
STILL = (1.0, 0.0, 0.0, 0.0, 2.5)
STATE_EDGES = ((8, 8, 16, 16), (0, 0, 8, 8))


def swap_near(cells):
    count = lax.axis_size("tile")
    return lax.ppermute(cells, "tile", [(i, i ^ 1) for i in range(count)])


def shift(cells, places):
    count = lax.axis_size("tile")
    return lax.ppermute(cells, "tile", [(i, (i + places) % count) for i in range(count)])


def swap_far(cells):
    count = lax.axis_size("tile")
    pairs = [(i, (i + (1 if i % 2 else -1)) % count) for i in range(count)]
    return lax.ppermute(cells, "tile", pairs)


def banded(ahead):
    weights = np.zeros(ahead.shape, np.float32)
    for places, weight in ((1, 8.0), (-1, -8.0), (2, -1.0), (-2, 1.0)):
        weights[ahead == places] = weight
    return weights


def second_weights():
    place = np.arange(LANES)
    ahead = (place[:, None] - place[None, :] + LANES // 2) % LANES - LANES // 2
    weights = banded(np.where(ahead % NZ == 0, ahead // NZ, LANES))
    return np.concatenate([weights, weights])


def first_weights(count, total, skip):
    weights = banded(np.arange(total)[None, :] - np.arange(count)[:, None] - skip)
    return np.concatenate([weights, weights], axis=1)


def all_weights(tall, span):
    sizes = {(tall - 2 * start, tall - 2 * start) for start in range(0, STEPS * SUB, SUB)}
    sizes |= {(tall - 2 * start - 2 * SUB, tall - 2 * start) for start in range(0, STEPS * SUB, SUB)}
    for edges in STATE_EDGES:
        sizes |= {(span - 2 * edges[n + 1], span - 2 * edges[n]) for n in range(3)}
    width = -(-2 * span // LANES) * LANES
    pieces, places, row = [], {}, 0
    second = second_weights()
    for piece, size in [(second, None)] + [(first_weights(*s, (s[1] - s[0]) // 2), s) for s in sorted(sizes)]:
        places[size] = row
        pieces.append(np.pad(piece, ((0, 0), (0, width - piece.shape[1]))))
        row += piece.shape[0]
    return np.concatenate(pieces), places


def parts(cells):
    high = cells.astype(jnp.bfloat16)
    return high, (cells - high.astype(jnp.float32)).astype(jnp.bfloat16)


def second_diff(high, low, weights):
    fields, count, _ = high.shape
    cells = jnp.concatenate([high, low], axis=2).reshape(fields * count, 2 * LANES)
    return jnp.dot(cells, weights, preferred_element_type=jnp.float32)


def first_diff(high, low, weights):
    cells = jnp.concatenate([high, low], axis=1)
    cells = jnp.concatenate([cells[k] for k in range(FIELDS)], axis=1)
    return jnp.dot(weights, cells, preferred_element_type=jnp.float32)


def lanes(k):
    return slice(k * LANES, (k + 1) * LANES)


def primitives(state):
    density, mom_x, mom_y, mom_z, energy = state
    inverse = 1.0 / density
    vel_x, vel_y, vel_z = mom_x * inverse, mom_y * inverse, mom_z * inverse
    half = 0.5 * (vel_x * vel_x + vel_y * vel_y + vel_z * vel_z)
    press = 0.4 * (energy - density * half)
    total = energy + press
    return vel_x, vel_y, vel_z, total * inverse, half, press, total


def together(works):
    done = object()
    while works:
        works = [work for work in works if next(work, done) is not done]


def tiles(start, stop):
    return [slice(place, place + SUB) for place in range(start, stop, SUB)]


def within(cells, rows, edge, span, k):
    if edge <= rows.start and rows.stop <= span - edge:
        return cells
    place = rows.start + lax.broadcasted_iota(jnp.int32, cells.shape, 0)
    return jnp.where(jnp.logical_and(place >= edge, place < span - edge), cells, STILL[k])


def state_stage(stage, moment, base_ref, coef_ref, now_ref, flux_ref, slope_ref, lefts, weights, span):
    here, there = STATE_EDGES[moment][stage], STATE_EDGES[moment][min(stage + 1, 3)]
    for rows in tiles(here, span - here):
        source_ref = base_ref if stage == 0 else now_ref
        state = [source_ref[moment, k, rows] for k in range(FIELDS)]
        vel_x, vel_y, vel_z, heat, half, press, total = primitives(state)
        for k, cells in enumerate((vel_x, vel_y, vel_z, heat, half)):
            coef_ref[moment, stage, k, rows] = cells
        if stage == 3:
            continue
        _, mom_x, mom_y, mom_z, _ = state
        cross = mom_x * vel_y
        first = (mom_x, mom_x * vel_x + press, cross, mom_z * vel_x, total * vel_x)
        second = (mom_y, cross, mom_y * vel_y + press, mom_z * vel_y, total * vel_y)
        for k in range(FIELDS):
            flux_ref[moment, k, rows] = first[k]
            if there <= rows.start < span - there:
                slope_ref[moment, k, rows] = second[k]
    if stage == 3:
        return
    count, total_rows = span - 2 * there, span - 2 * here
    left = lefts[count, total_rows]
    flux = flux_ref[moment, :, here : span - here]
    first = first_diff(*parts(flux), left)
    slope = slope_ref[moment, :, there : span - there]
    second = second_diff(*parts(slope), weights)
    second = second.reshape(FIELDS, count, LANES)
    yield
    scale = (0.5 if stage < 2 else 1.0) * twelfth
    for k in range(FIELDS):
        for rows in tiles(there, span - there):
            local_rows = slice(rows.start - there, rows.stop - there)
            slope = first[local_rows, lanes(k)] + second[k, local_rows]
            cells = base_ref[moment, k, rows] - scale * slope
            now_ref[moment, k, rows] = within(cells, rows, BASE_RIM - STATE_RIMS[moment] + 2 * (stage + 1), span, k)


def pull_differences(moment, stage, one, adj_ref, hold_ref, first_ref, second_ref, lefts, weights):
    tall = adj_ref.shape[2]
    start = (STEPS - 1 - moment) * SUB
    edge = start + SUB if stage == 0 else start
    source_ref = adj_ref if stage == 3 else hold_ref.at[2 - stage]
    total = tall - 2 * start
    high, low = parts(source_ref[one, :, start : tall - start])
    second = second_diff(high, low, weights).reshape(FIELDS, total, LANES)
    yield True
    first = first_diff(high, low, lefts[tall - 2 * edge, total])
    yield False
    for k in range(FIELDS):
        second_ref[one, k, start : tall - start] = second[k]
        yield True
        first_ref[one, edge : tall - edge, lanes(k)] = first[:, lanes(k)]
        yield True


def pull_stage(moment, stage, one, coef_ref, adj_ref, hold_ref, first_ref, second_ref, out_ref):
    tall = adj_ref.shape[2]
    shift, last = BASE_RIM - RIM, moment == 0
    start = (STEPS - 1 - moment) * SUB
    edge = start + SUB if stage == 0 else start
    for rows in tiles(edge, tall - edge):
        base_rows = slice(rows.start + shift, rows.stop + shift)
        vel_x, vel_y, vel_z, heat, half = [coef_ref[moment, stage, k, base_rows] for k in range(5)]
        a = [first_ref[one, rows, lanes(k)] for k in range(FIELDS)]
        b = [second_ref[one, k, rows] for k in range(FIELDS)]
        mix_x = vel_x * a[1] + vel_y * a[2] + vel_z * a[3] + heat * a[4]
        mix_y = vel_x * b[1] + vel_y * b[2] + vel_z * b[3] + heat * b[4]
        lift = vel_x * a[4] + vel_y * b[4]
        press = 0.4 * (a[1] + b[2] + lift)
        term = (
            half * press - vel_x * mix_x - vel_y * mix_y,
            a[0] + mix_x + vel_x * (a[1] - press) + vel_y * b[1],
            b[0] + mix_y + vel_y * (b[2] - press) + vel_x * a[2],
            vel_x * a[3] + vel_y * b[3] - vel_z * press,
            lift + press,
        )
        for k in range(FIELDS):
            adj = adj_ref[one, k, rows]
            if stage > 0:
                scale = (1.0 if stage == 1 else 0.5) * twelfth
                hold_ref[3 - stage, one, k, rows] = adj + scale * term[k]
                continue
            one_third, two_thirds, rest = [hold_ref[place, one, k, rows] for place in range(3)]
            mean = (one_third - adj + rest + 2.0 * two_thirds) * (1.0 / 3.0)
            result = mean + (twelfth / 6.0) * term[k]
            if last:
                out_ref[one, k, rows.start - RIM : rows.stop - RIM] = result
            else:
                adj_ref[one, k, rows] = result
        yield


def kernel(
    seeds_ref, near_ref, far_ref, blocks_ref, weights_ref, out_ref,
    adj_ref, hold_ref, first_ref, second_ref,
    base_ref, coef_ref, now_ref, flux_ref, slope_ref,
):
    funcs, _, strip, _ = seeds_ref.shape
    spread, _, block, _ = blocks_ref.shape
    tall, span = strip + 2 * RIM, strip + 2 * BASE_RIM
    even = lax.rem(lax.axis_index("tile"), 2) == 0

    def lay(left_ref, right_ref):
        for one in range(funcs):
            for k in range(FIELDS):
                adj_ref[one, k, :RIM] = left_ref[one, k]
                adj_ref[one, k, RIM + strip :] = right_ref[one, k]

    def lay_base(part, moment, shift, low, high):
        for owner in range(spread):
            start, stop = max(low, owner * block), min(high, (owner + 1) * block)
            if start < stop:
                rows = slice(start - owner * block, stop - owner * block)
                place = BASE_RIM + shift + start
                for k in range(FIELDS):
                    base_ref[moment, k, place : place + stop - start, :] = blocks_ref[owner, part * FIELDS + k, rows, :]

    for moment in range(STEPS):
        edge = BASE_RIM - STATE_RIMS[moment]
        for start in (STATE_EDGES[moment][0], span - STATE_EDGES[moment][0] - SUB):
            if start < edge or start + SUB > span - edge:
                for k in range(FIELDS):
                    base_ref[moment, k, start : start + SUB] = jnp.full((SUB, LANES), STILL[k], jnp.float32)
    middle = strip // 2
    lay_base(0, 0, 0, 0, strip)
    lay_base(1, 1, 0, 0, strip)
    lay_base(2, 1, strip, 0, middle)
    lay_base(2, 1, -strip, middle, strip)
    lay_base(3, 0, strip, 0, SHORT_RIM)
    lay_base(3, 1, -strip, max(SHORT_RIM, strip - LONG_RIM), middle)
    lay_base(3, 1, strip, middle, min(LONG_RIM, strip - SHORT_RIM))
    lay_base(3, 0, -strip, strip - SHORT_RIM, strip)

    _, places = all_weights(tall, span)
    weights = weights_ref[places[None] : places[None] + 2 * LANES, :LANES]
    lefts = {
        size: weights_ref[row : row + size[0], : 2 * size[1]] for size, row in places.items() if size is not None
    }

    def states(moment):
        for stage in range(4):
            yield from state_stage(
                stage, moment, base_ref, coef_ref, now_ref, flux_ref, slope_ref, lefts, weights, span
            )

    def differences(moment, stage, one):
        return pull_differences(moment, stage, one, adj_ref, hold_ref, first_ref, second_ref, lefts, weights)

    pl.when(even)(lambda: lay(far_ref, near_ref))
    pl.when(jnp.logical_not(even))(lambda: lay(near_ref, far_ref))
    for one in range(funcs):
        for k in range(FIELDS):
            adj_ref[one, k, RIM : RIM + strip] = seeds_ref[one, k]
    together([chain(*(differences(STEPS - 1, 3, one) for one in range(funcs))), states(1), states(0)])
    starting, storing = iter(()), iter(())
    for moment in reversed(range(STEPS)):
        for stage in (3, 2, 1, 0):
            for one in range(funcs):
                work = pull_stage(moment, stage, one, coef_ref, adj_ref, hold_ref, first_ref, second_ref, out_ref)
                begun = False
                for number, _ in enumerate(work):
                    if number % START_EVERY == 0 and not begun:
                        begun = next(starting, False) is False
                    for _ in range(STORES):
                        next(storing, None)
                while not begun:
                    begun = next(starting, False) is False
                for _ in storing:
                    pass
                storing, starting = starting, iter(())
                if stage > 0:
                    starting = differences(moment, stage - 1, one)
                elif moment > 0:
                    starting = differences(moment - 1, 3, one)


def local(seeds, checkpoints):
    funcs, _, strip, _ = seeds.shape
    block = checkpoints.shape[2]
    even = lax.rem(lax.axis_index("tile"), 2) == 0
    left, right = shift(checkpoints, 1), shift(checkpoints, -1)
    tail = strip - RIM
    far_edge = lax.dynamic_slice_in_dim(seeds, jnp.where(even, 0, tail), RIM, axis=2)
    near_edge = lax.dynamic_slice_in_dim(seeds, jnp.where(even, tail, 0), RIM, axis=2)
    own = checkpoints.reshape(STEPS * FIELDS, block, LANES)
    roomy = jnp.pad(own, ((0, STEPS * FIELDS), (0, 0), (0, 0)))
    roomy, right = lax.optimization_barrier((roomy, right))
    far, near = swap_far(far_edge), swap_near(near_edge)
    lower = lax.axis_index("func") * block < strip // 2
    main = lax.select(lower, right, left)
    other = lax.select(lower, left[1], right[1])
    place = lax.axis_index("func") * block + lax.broadcasted_iota(jnp.int32, (1, block, 1), 1)
    inner = jnp.logical_and(place >= SHORT_RIM, place < strip - SHORT_RIM)
    rest = jnp.where(inner, other, main[0])
    packed = lax.dynamic_update_slice(roomy, jnp.concatenate([main[1], rest], axis=0), (STEPS * FIELDS, 0, 0))
    blocks = lax.all_gather(packed, "func", axis=0, tiled=False)
    tall, span = strip + 2 * RIM, strip + 2 * BASE_RIM
    shapes = [
        (funcs, FIELDS, tall, LANES),
        (3, funcs, FIELDS, tall, LANES),
        (funcs, tall, FIELDS * LANES),
        (funcs, FIELDS, tall, LANES),
        (STEPS, FIELDS, span, LANES),
        (STEPS, 4, 5, span, LANES),
        (STEPS, FIELDS, span, LANES),
        (STEPS, FIELDS, span, LANES),
        (STEPS, FIELDS, span, LANES),
    ]
    vmem = pl.BlockSpec(memory_space=pltpu.VMEM)
    return pl.pallas_call(
        kernel,
        out_shape=jax.ShapeDtypeStruct(seeds.shape, jnp.float32),
        in_specs=[vmem] * 5,
        out_specs=vmem,
        scratch_shapes=[pltpu.VMEM(shape, jnp.float32) for shape in shapes],
        compiler_params=pltpu.CompilerParams(vmem_limit_bytes=32 * 1024 * 1024),
        name="two_steps",
    )(seeds, near, far, blocks, jnp.asarray(all_weights(tall, span)[0], jnp.bfloat16))


def solution(mesh):
    return jax.shard_map(
        local,
        mesh=mesh,
        in_specs=(P("func", None, "tile", None), P(None, None, ("tile", "func"), None)),
        out_specs=P("func", None, "tile", None),
        check_vma=False,
    )
```

```python
from itertools import chain

import jax
import jax.numpy as jnp
import numpy as np
from jax import lax
from jax.experimental import pallas as pl
from jax.experimental.pallas import tpu as pltpu
from jax.sharding import PartitionSpec as P

NZ = 4
STEPS = 2
FIELDS = 5
LANES = 128
SUB = 8

step_size = 0.3
twelfth = step_size / 12.0

RIM = 16
BASE_RIM = 24
LONG_RIM = 20
SHORT_RIM = 12
STATE_RIMS = (SHORT_RIM, LONG_RIM)
START_EVERY, STORES = 2, 2
STILL = (1.0, 0.0, 0.0, 0.0, 2.5)
STATE_EDGES = ((8, 8, 16, 16), (0, 0, 8, 8))


def swap_near(cells):
    count = lax.axis_size("tile")
    return lax.ppermute(cells, "tile", [(i, i ^ 1) for i in range(count)])


def shift(cells, places):
    count = lax.axis_size("tile")
    return lax.ppermute(cells, "tile", [(i, (i + places) % count) for i in range(count)])


def swap_far(cells):
    count = lax.axis_size("tile")
    pairs = [(i, (i + (1 if i % 2 else -1)) % count) for i in range(count)]
    return lax.ppermute(cells, "tile", pairs)


def banded(ahead):
    weights = np.zeros(ahead.shape, np.float32)
    for places, weight in ((1, 8.0), (-1, -8.0), (2, -1.0), (-2, 1.0)):
        weights[ahead == places] = weight
    return weights


def second_weights():
    place = np.arange(LANES)
    ahead = (place[:, None] - place[None, :] + LANES // 2) % LANES - LANES // 2
    weights = banded(np.where(ahead % NZ == 0, ahead // NZ, LANES))
    return np.concatenate([weights, weights])


def first_weights(count, total, skip):
    weights = banded(np.arange(total)[None, :] - np.arange(count)[:, None] - skip)
    return np.concatenate([weights, weights], axis=1)


def all_weights(tall, span):
    sizes = {(tall - 2 * start, tall - 2 * start) for start in range(0, STEPS * SUB, SUB)}
    sizes |= {(tall - 2 * start - 2 * SUB, tall - 2 * start) for start in range(0, STEPS * SUB, SUB)}
    for edges in STATE_EDGES:
        sizes |= {(span - 2 * edges[n + 1], span - 2 * edges[n]) for n in range(3)}
    width = -(-2 * span // LANES) * LANES
    pieces, places, row = [], {}, 0
    second = second_weights()
    for piece, size in [(second, None)] + [(first_weights(*s, (s[1] - s[0]) // 2), s) for s in sorted(sizes)]:
        places[size] = row
        pieces.append(np.pad(piece, ((0, 0), (0, width - piece.shape[1]))))
        row += piece.shape[0]
    return np.concatenate(pieces), places


def parts(cells):
    high = cells.astype(jnp.bfloat16)
    return high, (cells - high.astype(jnp.float32)).astype(jnp.bfloat16)


def second_diff(high, low, weights):
    fields, count, _ = high.shape
    cells = jnp.concatenate([high, low], axis=2).reshape(fields * count, 2 * LANES)
    return jnp.dot(cells, weights, preferred_element_type=jnp.float32)


def first_diff(high, low, weights):
    cells = jnp.concatenate([high, low], axis=1)
    cells = jnp.concatenate([cells[k] for k in range(FIELDS)], axis=1)
    return jnp.dot(weights, cells, preferred_element_type=jnp.float32)


def lanes(k):
    return slice(k * LANES, (k + 1) * LANES)


def primitives(state):
    density, mom_x, mom_y, mom_z, energy = state
    inverse = 1.0 / density
    vel_x, vel_y, vel_z = mom_x * inverse, mom_y * inverse, mom_z * inverse
    half = 0.5 * (vel_x * vel_x + vel_y * vel_y + vel_z * vel_z)
    press = 0.4 * (energy - density * half)
    total = energy + press
    return vel_x, vel_y, vel_z, total * inverse, half, press, total


def together(works):
    done = object()
    while works:
        works = [work for work in works if next(work, done) is not done]


def tiles(start, stop):
    return [slice(place, place + SUB) for place in range(start, stop, SUB)]


def within(cells, rows, edge, span, k):
    if edge <= rows.start and rows.stop <= span - edge:
        return cells
    place = rows.start + lax.broadcasted_iota(jnp.int32, cells.shape, 0)
    return jnp.where(jnp.logical_and(place >= edge, place < span - edge), cells, STILL[k])


def state_stage(stage, moment, base_ref, coef_ref, now_ref, flux_ref, slope_ref, lefts, weights, span):
    here, there = STATE_EDGES[moment][stage], STATE_EDGES[moment][min(stage + 1, 3)]
    for rows in tiles(here, span - here):
        source_ref = base_ref if stage == 0 else now_ref
        state = [source_ref[moment, k, rows] for k in range(FIELDS)]
        vel_x, vel_y, vel_z, heat, half, press, total = primitives(state)
        for k, cells in enumerate((vel_x, vel_y, vel_z, heat, half)):
            coef_ref[moment, stage, k, rows] = cells
        if stage == 3:
            continue
        _, mom_x, mom_y, mom_z, _ = state
        cross = mom_x * vel_y
        first = (mom_x, mom_x * vel_x + press, cross, mom_z * vel_x, total * vel_x)
        second = (mom_y, cross, mom_y * vel_y + press, mom_z * vel_y, total * vel_y)
        for k in range(FIELDS):
            flux_ref[moment, k, rows] = first[k]
            if there <= rows.start < span - there:
                slope_ref[moment, k, rows] = second[k]
    if stage == 3:
        return
    count, total_rows = span - 2 * there, span - 2 * here
    left = lefts[count, total_rows]
    flux = flux_ref[moment, :, here : span - here]
    first = first_diff(*parts(flux), left)
    slope = slope_ref[moment, :, there : span - there]
    second = second_diff(*parts(slope), weights)
    second = second.reshape(FIELDS, count, LANES)
    yield
    scale = (0.5 if stage < 2 else 1.0) * twelfth
    for k in range(FIELDS):
        for rows in tiles(there, span - there):
            local_rows = slice(rows.start - there, rows.stop - there)
            slope = first[local_rows, lanes(k)] + second[k, local_rows]
            cells = base_ref[moment, k, rows] - scale * slope
            now_ref[moment, k, rows] = within(cells, rows, BASE_RIM - STATE_RIMS[moment] + 2 * (stage + 1), span, k)


def pull_differences(moment, stage, one, adj_ref, hold_ref, first_ref, second_ref, lefts, weights):
    tall = adj_ref.shape[2]
    start = (STEPS - 1 - moment) * SUB
    edge = start + SUB if stage == 0 else start
    source_ref = adj_ref if stage == 3 else hold_ref.at[2 - stage]
    total = tall - 2 * start
    high, low = parts(source_ref[one, :, start : tall - start])
    second = second_diff(high, low, weights).reshape(FIELDS, total, LANES)
    yield True
    first = first_diff(high, low, lefts[tall - 2 * edge, total])
    yield False
    for k in range(FIELDS):
        second_ref[one, k, start : tall - start] = second[k]
        yield True
        first_ref[one, edge : tall - edge, lanes(k)] = first[:, lanes(k)]
        yield True


def pull_stage(moment, stage, one, coef_ref, adj_ref, hold_ref, first_ref, second_ref, out_ref):
    tall = adj_ref.shape[2]
    shift, last = BASE_RIM - RIM, moment == 0
    start = (STEPS - 1 - moment) * SUB
    edge = start + SUB if stage == 0 else start
    for rows in tiles(edge, tall - edge):
        base_rows = slice(rows.start + shift, rows.stop + shift)
        vel_x, vel_y, vel_z, heat, half = [coef_ref[moment, stage, k, base_rows] for k in range(5)]
        a = [first_ref[one, rows, lanes(k)] for k in range(FIELDS)]
        b = [second_ref[one, k, rows] for k in range(FIELDS)]
        mix_x = vel_x * a[1] + vel_y * a[2] + vel_z * a[3] + heat * a[4]
        mix_y = vel_x * b[1] + vel_y * b[2] + vel_z * b[3] + heat * b[4]
        lift = vel_x * a[4] + vel_y * b[4]
        press = 0.4 * (a[1] + b[2] + lift)
        term = (
            half * press - vel_x * mix_x - vel_y * mix_y,
            a[0] + mix_x + vel_x * (a[1] - press) + vel_y * b[1],
            b[0] + mix_y + vel_y * (b[2] - press) + vel_x * a[2],
            vel_x * a[3] + vel_y * b[3] - vel_z * press,
            lift + press,
        )
        for k in range(FIELDS):
            adj = adj_ref[one, k, rows]
            if stage > 0:
                scale = (1.0 if stage == 1 else 0.5) * twelfth
                hold_ref[3 - stage, one, k, rows] = adj + scale * term[k]
                continue
            one_third, two_thirds, rest = [hold_ref[place, one, k, rows] for place in range(3)]
            mean = (one_third - adj + rest + 2.0 * two_thirds) * (1.0 / 3.0)
            result = mean + (twelfth / 6.0) * term[k]
            if last:
                out_ref[one, k, rows.start - RIM : rows.stop - RIM] = result
            else:
                adj_ref[one, k, rows] = result
        yield


def kernel(
    seeds_ref, near_ref, far_ref, blocks_ref, weights_ref, out_ref,
    adj_ref, hold_ref, first_ref, second_ref,
    base_ref, coef_ref, now_ref, flux_ref, slope_ref,
):
    funcs, _, strip, _ = seeds_ref.shape
    spread, _, block, _ = blocks_ref.shape
    tall, span = strip + 2 * RIM, strip + 2 * BASE_RIM
    even = lax.rem(lax.axis_index("tile"), 2) == 0

    def lay_base(part, moment, shift, low, high):
        for owner in range(spread):
            start, stop = max(low, owner * block), min(high, (owner + 1) * block)
            if start < stop:
                rows = slice(start - owner * block, stop - owner * block)
                place = BASE_RIM + shift + start
                for k in range(FIELDS):
                    base_ref[moment, k, place : place + stop - start, :] = blocks_ref[owner, part * FIELDS + k, rows, :]

    for moment in range(STEPS):
        edge = BASE_RIM - STATE_RIMS[moment]
        for start in (STATE_EDGES[moment][0], span - STATE_EDGES[moment][0] - SUB):
            if start < edge or start + SUB > span - edge:
                for k in range(FIELDS):
                    base_ref[moment, k, start : start + SUB] = jnp.full((SUB, LANES), STILL[k], jnp.float32)
    middle = strip // 2
    lay_base(0, 0, 0, 0, strip)
    lay_base(1, 1, 0, 0, strip)
    lay_base(2, 1, strip, 0, middle)
    lay_base(2, 1, -strip, middle, strip)
    lay_base(3, 0, strip, 0, SHORT_RIM)
    lay_base(3, 1, -strip, max(SHORT_RIM, strip - LONG_RIM), middle)
    lay_base(3, 1, strip, middle, min(LONG_RIM, strip - SHORT_RIM))
    lay_base(3, 0, -strip, strip - SHORT_RIM, strip)

    _, places = all_weights(tall, span)
    weights = weights_ref[places[None] : places[None] + 2 * LANES, :LANES]
    lefts = {
        size: weights_ref[row : row + size[0], : 2 * size[1]] for size, row in places.items() if size is not None
    }

    def states(moment):
        for stage in range(4):
            yield from state_stage(
                stage, moment, base_ref, coef_ref, now_ref, flux_ref, slope_ref, lefts, weights, span
            )

    def differences(moment, stage, one):
        return pull_differences(moment, stage, one, adj_ref, hold_ref, first_ref, second_ref, lefts, weights)

    for one in range(funcs):
        for k in range(FIELDS):
            near, far = near_ref[one, k], far_ref[one, k]
            adj_ref[one, k, :RIM] = jnp.where(even, far, near)
            adj_ref[one, k, RIM + strip :] = jnp.where(even, near, far)
    for one in range(funcs):
        for k in range(FIELDS):
            adj_ref[one, k, RIM : RIM + strip] = seeds_ref[one, k]
    together([chain(*(differences(STEPS - 1, 3, one) for one in range(funcs))), states(1), states(0)])
    starting, storing = iter(()), iter(())
    for moment in reversed(range(STEPS)):
        for stage in (3, 2, 1, 0):
            for one in range(funcs):
                work = pull_stage(moment, stage, one, coef_ref, adj_ref, hold_ref, first_ref, second_ref, out_ref)
                begun = False
                for number, _ in enumerate(work):
                    if number % START_EVERY == 0 and not begun:
                        begun = next(starting, False) is False
                    for _ in range(STORES):
                        next(storing, None)
                while not begun:
                    begun = next(starting, False) is False
                for _ in storing:
                    pass
                storing, starting = starting, iter(())
                if stage > 0:
                    starting = differences(moment, stage - 1, one)
                elif moment > 0:
                    starting = differences(moment - 1, 3, one)


def local(seeds, checkpoints):
    funcs, _, strip, _ = seeds.shape
    block = checkpoints.shape[2]
    even = lax.rem(lax.axis_index("tile"), 2) == 0
    left, right = shift(checkpoints, 1), shift(checkpoints, -1)
    tail = strip - RIM
    far_edge = lax.dynamic_slice_in_dim(seeds, jnp.where(even, 0, tail), RIM, axis=2)
    near_edge = lax.dynamic_slice_in_dim(seeds, jnp.where(even, tail, 0), RIM, axis=2)
    own = checkpoints.reshape(STEPS * FIELDS, block, LANES)
    roomy = jnp.pad(own, ((0, STEPS * FIELDS), (0, 0), (0, 0)))
    roomy, right = lax.optimization_barrier((roomy, right))
    far, near = swap_far(far_edge), swap_near(near_edge)
    lower = lax.axis_index("func") * block < strip // 2
    main = lax.select(lower, right, left)
    other = lax.select(lower, left[1], right[1])
    place = lax.axis_index("func") * block + lax.broadcasted_iota(jnp.int32, (1, block, 1), 1)
    inner = jnp.logical_and(place >= SHORT_RIM, place < strip - SHORT_RIM)
    rest = jnp.where(inner, other, main[0])
    packed = lax.dynamic_update_slice(roomy, jnp.concatenate([main[1], rest], axis=0), (STEPS * FIELDS, 0, 0))
    blocks = lax.all_gather(packed, "func", axis=0, tiled=False)
    tall, span = strip + 2 * RIM, strip + 2 * BASE_RIM
    shapes = [
        (funcs, FIELDS, tall, LANES),
        (3, funcs, FIELDS, tall, LANES),
        (funcs, tall, FIELDS * LANES),
        (funcs, FIELDS, tall, LANES),
        (STEPS, FIELDS, span, LANES),
        (STEPS, 4, 5, span, LANES),
        (STEPS, FIELDS, span, LANES),
        (STEPS, FIELDS, span, LANES),
        (STEPS, FIELDS, span, LANES),
    ]
    vmem = pl.BlockSpec(memory_space=pltpu.VMEM)
    return pl.pallas_call(
        kernel,
        out_shape=jax.ShapeDtypeStruct(seeds.shape, jnp.float32),
        in_specs=[vmem] * 5,
        out_specs=vmem,
        scratch_shapes=[pltpu.VMEM(shape, jnp.float32) for shape in shapes],
        compiler_params=pltpu.CompilerParams(vmem_limit_bytes=32 * 1024 * 1024),
        name="two_steps",
    )(seeds, near, far, blocks, jnp.asarray(all_weights(tall, span)[0], jnp.bfloat16))


def solution(mesh):
    return jax.shard_map(
        local,
        mesh=mesh,
        in_specs=(P("func", None, "tile", None), P(None, None, ("tile", "func"), None)),
        out_specs=P("func", None, "tile", None),
        check_vma=False,
    )
```

```python
from itertools import chain

import jax
import jax.numpy as jnp
import numpy as np
from jax import lax
from jax.experimental import pallas as pl
from jax.experimental.pallas import tpu as pltpu
from jax.sharding import PartitionSpec as P

NZ = 4
STEPS = 2
FIELDS = 5
LANES = 128
SUB = 8

step_size = 0.3
twelfth = step_size / 12.0

RIM = 16
BASE_RIM = 24
LONG_RIM = 20
SHORT_RIM = 12
STATE_RIMS = (SHORT_RIM, LONG_RIM)
START_EVERY, STORES = 2, 1
STILL = (1.0, 0.0, 0.0, 0.0, 2.5)
STATE_EDGES = ((8, 8, 16, 16), (0, 0, 8, 8))


def swap_near(cells):
    count = lax.axis_size("tile")
    return lax.ppermute(cells, "tile", [(i, i ^ 1) for i in range(count)])


def shift(cells, places):
    count = lax.axis_size("tile")
    return lax.ppermute(cells, "tile", [(i, (i + places) % count) for i in range(count)])


def swap_far(cells):
    count = lax.axis_size("tile")
    pairs = [(i, (i + (1 if i % 2 else -1)) % count) for i in range(count)]
    return lax.ppermute(cells, "tile", pairs)


def banded(ahead):
    weights = np.zeros(ahead.shape, np.float32)
    for places, weight in ((1, 8.0), (-1, -8.0), (2, -1.0), (-2, 1.0)):
        weights[ahead == places] = weight
    return weights


def second_weights():
    place = np.arange(LANES)
    ahead = (place[:, None] - place[None, :] + LANES // 2) % LANES - LANES // 2
    weights = banded(np.where(ahead % NZ == 0, ahead // NZ, LANES))
    return np.concatenate([weights, weights])


def first_weights(count, total, skip):
    weights = banded(np.arange(total)[None, :] - np.arange(count)[:, None] - skip)
    return np.concatenate([weights, weights], axis=1)


def all_weights(tall, span):
    sizes = {(tall - 2 * start, tall - 2 * start) for start in range(0, STEPS * SUB, SUB)}
    sizes |= {(tall - 2 * start - 2 * SUB, tall - 2 * start) for start in range(0, STEPS * SUB, SUB)}
    for edges in STATE_EDGES:
        sizes |= {(span - 2 * edges[n + 1], span - 2 * edges[n]) for n in range(3)}
    width = -(-2 * span // LANES) * LANES
    pieces, places, row = [], {}, 0
    second = second_weights()
    for piece, size in [(second, None)] + [(first_weights(*s, (s[1] - s[0]) // 2), s) for s in sorted(sizes)]:
        places[size] = row
        pieces.append(np.pad(piece, ((0, 0), (0, width - piece.shape[1]))))
        row += piece.shape[0]
    return np.concatenate(pieces), places


def parts(cells):
    high = cells.astype(jnp.bfloat16)
    return high, (cells - high.astype(jnp.float32)).astype(jnp.bfloat16)


def second_diff(high, low, weights):
    fields, count, _ = high.shape
    cells = jnp.concatenate([high, low], axis=2).reshape(fields * count, 2 * LANES)
    return jnp.dot(cells, weights, preferred_element_type=jnp.float32)


def first_diff(high, low, weights):
    cells = jnp.concatenate([high, low], axis=1)
    cells = jnp.concatenate([cells[k] for k in range(FIELDS)], axis=1)
    return jnp.dot(weights, cells, preferred_element_type=jnp.float32)


def lanes(k):
    return slice(k * LANES, (k + 1) * LANES)


def primitives(state):
    density, mom_x, mom_y, mom_z, energy = state
    inverse = 1.0 / density
    vel_x, vel_y, vel_z = mom_x * inverse, mom_y * inverse, mom_z * inverse
    half = 0.5 * (vel_x * vel_x + vel_y * vel_y + vel_z * vel_z)
    press = 0.4 * (energy - density * half)
    total = energy + press
    return vel_x, vel_y, vel_z, total * inverse, half, press, total


def together(works):
    done = object()
    while works:
        works = [work for work in works if next(work, done) is not done]


def tiles(start, stop):
    return [slice(place, place + SUB) for place in range(start, stop, SUB)]


def within(cells, rows, edge, span, k):
    if edge <= rows.start and rows.stop <= span - edge:
        return cells
    place = rows.start + lax.broadcasted_iota(jnp.int32, cells.shape, 0)
    return jnp.where(jnp.logical_and(place >= edge, place < span - edge), cells, STILL[k])


def state_stage(stage, moment, base_ref, coef_ref, now_ref, flux_ref, slope_ref, lefts, weights, span):
    here, there = STATE_EDGES[moment][stage], STATE_EDGES[moment][min(stage + 1, 3)]
    for rows in tiles(here, span - here):
        source_ref = base_ref if stage == 0 else now_ref
        state = [source_ref[moment, k, rows] for k in range(FIELDS)]
        vel_x, vel_y, vel_z, heat, half, press, total = primitives(state)
        for k, cells in enumerate((vel_x, vel_y, vel_z, heat, half)):
            coef_ref[moment, stage, k, rows] = cells
        if stage == 3:
            continue
        _, mom_x, mom_y, mom_z, _ = state
        cross = mom_x * vel_y
        first = (mom_x, mom_x * vel_x + press, cross, mom_z * vel_x, total * vel_x)
        second = (mom_y, cross, mom_y * vel_y + press, mom_z * vel_y, total * vel_y)
        for k in range(FIELDS):
            flux_ref[moment, k, rows] = first[k]
            if there <= rows.start < span - there:
                slope_ref[moment, k, rows] = second[k]
    if stage == 3:
        return
    count, total_rows = span - 2 * there, span - 2 * here
    left = lefts[count, total_rows]
    flux = flux_ref[moment, :, here : span - here]
    first = first_diff(*parts(flux), left)
    slope = slope_ref[moment, :, there : span - there]
    second = second_diff(*parts(slope), weights)
    second = second.reshape(FIELDS, count, LANES)
    yield
    scale = (0.5 if stage < 2 else 1.0) * twelfth
    for k in range(FIELDS):
        for rows in tiles(there, span - there):
            local_rows = slice(rows.start - there, rows.stop - there)
            slope = first[local_rows, lanes(k)] + second[k, local_rows]
            cells = base_ref[moment, k, rows] - scale * slope
            now_ref[moment, k, rows] = within(cells, rows, BASE_RIM - STATE_RIMS[moment] + 2 * (stage + 1), span, k)


def pull_differences(moment, stage, one, adj_ref, hold_ref, first_ref, second_ref, lefts, weights):
    tall = adj_ref.shape[2]
    start = (STEPS - 1 - moment) * SUB
    edge = start + SUB if stage == 0 else start
    source_ref = adj_ref if stage == 3 else hold_ref.at[2 - stage]
    total = tall - 2 * start
    high, low = parts(source_ref[one, :, start : tall - start])
    second = second_diff(high, low, weights).reshape(FIELDS, total, LANES)
    yield True
    first = first_diff(high, low, lefts[tall - 2 * edge, total])
    yield False
    for k in range(FIELDS):
        second_ref[one, k, start : tall - start] = second[k]
        yield True
        first_ref[one, edge : tall - edge, lanes(k)] = first[:, lanes(k)]
        yield True


def pull_stage(moment, stage, one, coef_ref, adj_ref, hold_ref, first_ref, second_ref, out_ref):
    tall = adj_ref.shape[2]
    shift, last = BASE_RIM - RIM, moment == 0
    start = (STEPS - 1 - moment) * SUB
    edge = start + SUB if stage == 0 else start
    for rows in tiles(edge, tall - edge):
        base_rows = slice(rows.start + shift, rows.stop + shift)
        vel_x, vel_y, vel_z, heat, half = [coef_ref[moment, stage, k, base_rows] for k in range(5)]
        a = [first_ref[one, rows, lanes(k)] for k in range(FIELDS)]
        b = [second_ref[one, k, rows] for k in range(FIELDS)]
        mix_x = vel_x * a[1] + vel_y * a[2] + vel_z * a[3] + heat * a[4]
        mix_y = vel_x * b[1] + vel_y * b[2] + vel_z * b[3] + heat * b[4]
        lift = vel_x * a[4] + vel_y * b[4]
        press = 0.4 * (a[1] + b[2] + lift)
        term = (
            half * press - vel_x * mix_x - vel_y * mix_y,
            a[0] + mix_x + vel_x * (a[1] - press) + vel_y * b[1],
            b[0] + mix_y + vel_y * (b[2] - press) + vel_x * a[2],
            vel_x * a[3] + vel_y * b[3] - vel_z * press,
            lift + press,
        )
        for k in range(FIELDS):
            adj = adj_ref[one, k, rows]
            if stage > 0:
                scale = (1.0 if stage == 1 else 0.5) * twelfth
                hold_ref[3 - stage, one, k, rows] = adj + scale * term[k]
                continue
            one_third, two_thirds, rest = [hold_ref[place, one, k, rows] for place in range(3)]
            mean = (one_third - adj + rest + 2.0 * two_thirds) * (1.0 / 3.0)
            result = mean + (twelfth / 6.0) * term[k]
            if last:
                out_ref[one, k, rows.start - RIM : rows.stop - RIM] = result
            else:
                adj_ref[one, k, rows] = result
        yield


def kernel(
    seeds_ref, near_ref, far_ref, blocks_ref, weights_ref, out_ref,
    adj_ref, hold_ref, first_ref, second_ref,
    base_ref, coef_ref, now_ref, flux_ref, slope_ref,
):
    funcs, _, strip, _ = seeds_ref.shape
    spread, _, block, _ = blocks_ref.shape
    tall, span = strip + 2 * RIM, strip + 2 * BASE_RIM
    even = lax.rem(lax.axis_index("tile"), 2) == 0

    def lay_base(part, moment, shift, low, high):
        for owner in range(spread):
            start, stop = max(low, owner * block), min(high, (owner + 1) * block)
            if start < stop:
                rows = slice(start - owner * block, stop - owner * block)
                place = BASE_RIM + shift + start
                for k in range(FIELDS):
                    base_ref[moment, k, place : place + stop - start, :] = blocks_ref[owner, part * FIELDS + k, rows, :]

    for moment in range(STEPS):
        edge = BASE_RIM - STATE_RIMS[moment]
        for start in (STATE_EDGES[moment][0], span - STATE_EDGES[moment][0] - SUB):
            if start < edge or start + SUB > span - edge:
                for k in range(FIELDS):
                    base_ref[moment, k, start : start + SUB] = jnp.full((SUB, LANES), STILL[k], jnp.float32)
    middle = strip // 2
    lay_base(0, 0, 0, 0, strip)
    lay_base(1, 1, 0, 0, strip)
    lay_base(2, 1, strip, 0, middle)
    lay_base(2, 1, -strip, middle, strip)
    lay_base(3, 0, strip, 0, SHORT_RIM)
    lay_base(3, 1, -strip, max(SHORT_RIM, strip - LONG_RIM), middle)
    lay_base(3, 1, strip, middle, min(LONG_RIM, strip - SHORT_RIM))
    lay_base(3, 0, -strip, strip - SHORT_RIM, strip)

    _, places = all_weights(tall, span)
    weights = weights_ref[places[None] : places[None] + 2 * LANES, :LANES]
    lefts = {
        size: weights_ref[row : row + size[0], : 2 * size[1]] for size, row in places.items() if size is not None
    }

    def states(moment):
        for stage in range(4):
            yield from state_stage(
                stage, moment, base_ref, coef_ref, now_ref, flux_ref, slope_ref, lefts, weights, span
            )

    def differences(moment, stage, one):
        return pull_differences(moment, stage, one, adj_ref, hold_ref, first_ref, second_ref, lefts, weights)

    for one in range(funcs):
        for k in range(FIELDS):
            near, far = near_ref[one, k], far_ref[one, k]
            adj_ref[one, k, :RIM] = jnp.where(even, far, near)
            adj_ref[one, k, RIM + strip :] = jnp.where(even, near, far)
    for one in range(funcs):
        for k in range(FIELDS):
            adj_ref[one, k, RIM : RIM + strip] = seeds_ref[one, k]
    together([chain(*(differences(STEPS - 1, 3, one) for one in range(funcs))), states(1), states(0)])
    starting, storing = iter(()), iter(())
    for moment in reversed(range(STEPS)):
        for stage in (3, 2, 1, 0):
            for one in range(funcs):
                work = pull_stage(moment, stage, one, coef_ref, adj_ref, hold_ref, first_ref, second_ref, out_ref)
                begun = False
                for number, _ in enumerate(work):
                    if number % START_EVERY == 0 and not begun:
                        begun = next(starting, False) is False
                    for _ in range(STORES):
                        next(storing, None)
                while not begun:
                    begun = next(starting, False) is False
                for _ in storing:
                    pass
                storing, starting = starting, iter(())
                if stage > 0:
                    starting = differences(moment, stage - 1, one)
                elif moment > 0:
                    starting = differences(moment - 1, 3, one)


def local(seeds, checkpoints):
    funcs, _, strip, _ = seeds.shape
    block = checkpoints.shape[2]
    even = lax.rem(lax.axis_index("tile"), 2) == 0
    left, right = shift(checkpoints, 1), shift(checkpoints, -1)
    tail = strip - RIM
    far_edge = lax.dynamic_slice_in_dim(seeds, jnp.where(even, 0, tail), RIM, axis=2)
    near_edge = lax.dynamic_slice_in_dim(seeds, jnp.where(even, tail, 0), RIM, axis=2)
    own = checkpoints.reshape(STEPS * FIELDS, block, LANES)
    roomy = jnp.pad(own, ((0, STEPS * FIELDS), (0, 0), (0, 0)))
    roomy, right = lax.optimization_barrier((roomy, right))
    far, near = swap_far(far_edge), swap_near(near_edge)
    lower = lax.axis_index("func") * block < strip // 2
    main = lax.select(lower, right, left)
    other = lax.select(lower, left[1], right[1])
    place = lax.axis_index("func") * block + lax.broadcasted_iota(jnp.int32, (1, block, 1), 1)
    inner = jnp.logical_and(place >= SHORT_RIM, place < strip - SHORT_RIM)
    rest = jnp.where(inner, other, main[0])
    packed = lax.dynamic_update_slice(roomy, jnp.concatenate([main[1], rest], axis=0), (STEPS * FIELDS, 0, 0))
    blocks = lax.all_gather(packed, "func", axis=0, tiled=False)
    tall, span = strip + 2 * RIM, strip + 2 * BASE_RIM
    shapes = [
        (funcs, FIELDS, tall, LANES),
        (3, funcs, FIELDS, tall, LANES),
        (funcs, tall, FIELDS * LANES),
        (funcs, FIELDS, tall, LANES),
        (STEPS, FIELDS, span, LANES),
        (STEPS, 4, 5, span, LANES),
        (STEPS, FIELDS, span, LANES),
        (STEPS, FIELDS, span, LANES),
        (STEPS, FIELDS, span, LANES),
    ]
    vmem = pl.BlockSpec(memory_space=pltpu.VMEM)
    return pl.pallas_call(
        kernel,
        out_shape=jax.ShapeDtypeStruct(seeds.shape, jnp.float32),
        in_specs=[vmem] * 5,
        out_specs=vmem,
        scratch_shapes=[pltpu.VMEM(shape, jnp.float32) for shape in shapes],
        compiler_params=pltpu.CompilerParams(vmem_limit_bytes=32 * 1024 * 1024),
        name="two_steps",
    )(seeds, near, far, blocks, jnp.asarray(all_weights(tall, span)[0], jnp.bfloat16))


def solution(mesh):
    return jax.shard_map(
        local,
        mesh=mesh,
        in_specs=(P("func", None, "tile", None), P(None, None, ("tile", "func"), None)),
        out_specs=P("func", None, "tile", None),
        check_vma=False,
    )
```
